32 devices in a mesh: gx: 2 (over x), gy: 8 (over z, core), gz: 2 (over y).
Axes of the slice: x: 2, y: 2, z: 4, core: 2. Of those that a mesh axis runs over, the one named last changes fastest.
Arguments:
- forward_e: bfloat16 [3, 64, 128, 512], P(None, 'gz', 'gy', 'gx'), may hold values from -3 to 3
- forward_h: bfloat16 [3, 64, 128, 512], P(None, 'gz', 'gy', 'gx'), may hold values from -3 to 3
- adjoint_e: bfloat16 [3, 64, 128, 512], P(None, 'gz', 'gy', 'gx'), may hold values from -3 to 3
- adjoint_h: bfloat16 [3, 64, 128, 512], P(None, 'gz', 'gy', 'gx'), may hold values from -3 to 3
- material: int32 [64, 128, 512], P('gz', 'gy', 'gx'), may hold values from 0 to 3
- inv_permittivity: float32 [4], replicated, may hold values from 0.15 to 1
- height: int32 [128, 512], P('gy', 'gx'), may hold values from 0 to 64
Outputs:
- column_grad: float32 [128, 512], P('gy', 'gx')
- dual_h: float32 [3, 64, 128, 512], P(None, 'gz', 'gy', 'gx')
The draws below stay inside these ranges and needn't reach their ends.
All inputs are finite; a program needn't handle non-finite values.
Results may differ from the reference program's by a relative error of at most 0.0003.
Values sent between devices are 32-bit elements; how exact they have to be, the bound alone decides.
No kernel may reach another device: no remote copies, remote signals or barrier semaphores. Data moves between devices by JAX's collectives and lax.ppermute only.
A program may use at most 320 MiB of HBM per device.

```python
import math
import jax
import jax.numpy as jnp
from jax import lax

STEPS = 3
MATERIALS = 4
NX = 512
NY = 128
NZ = 64


def touch_ends(values, rng, least, high):
    spot = [jax.random.randint(jax.random.fold_in(rng, axis), (), 0, length) for axis, length in enumerate(values.shape)]
    longest = values.shape.index(max(values.shape))
    next_to = spot[:longest] + [(spot[longest] + 1) % values.shape[longest]] + spot[longest + 1:]
    return values.at[tuple(spot)].set(least).at[tuple(next_to)].set(high)


def level_of(key, extent, cuts, smallest, top_value):
    level, own = 1.0, jax.random.fold_in(key, 6)
    for position, parts in cuts:
        heights = jnp.exp(jax.random.uniform(jax.random.fold_in(own, position), (parts,), jnp.float32, smallest / len(cuts), top_value / len(cuts)))
        level = level * jnp.repeat(heights, extent[position] // parts).reshape([-1 if axis == position else 1 for axis in range(len(extent))])
    return level


def gaussian(stream_key, dims, deviation, reach, shards=(), kind=jnp.bfloat16):
    array = deviation * jax.random.normal(stream_key, dims, jnp.float32)
    if shards:
        array = array * level_of(stream_key, dims, shards, -0.22, 0.18)
    return jnp.clip(array, -reach, reach).astype(kind)


def setup_inputs(seed: int = 0) -> dict:
    seeds = jax.random.split(jax.random.key(seed), 8)
    forward_e = gaussian(seeds[0], (3, NZ, NY, NX), 0.5, 3.0, ((1, 2), (2, 8), (3, 2)))
    forward_h = gaussian(seeds[1], (3, NZ, NY, NX), 0.5, 3.0, ((1, 2), (2, 8), (3, 2)))
    adjoint_e = gaussian(seeds[2], (3, NZ, NY, NX), 0.5, 3.0, ((1, 2), (2, 8), (3, 2)))
    adjoint_h = gaussian(seeds[3], (3, NZ, NY, NX), 0.5, 3.0, ((1, 2), (2, 8), (3, 2)))
    material = touch_ends(jax.random.randint(seeds[4], (NZ, NY, NX), 0, MATERIALS), jax.random.fold_in(seeds[4], 1), 0, MATERIALS - 1).astype(jnp.int32)
    inv_permittivity = jnp.clip(jnp.exp(jax.random.uniform(seeds[5], (MATERIALS,), jnp.float32, math.log(0.15), math.log(1.0))), 0.15, 1.0)
    height = touch_ends(jax.random.randint(seeds[6], (NY, NX), 0, NZ + 1), jax.random.fold_in(seeds[6], 1), 0, NZ).astype(jnp.int32)
    return dict(forward_e=forward_e, forward_h=forward_h, adjoint_e=adjoint_e, adjoint_h=adjoint_h, material=material, inv_permittivity=inv_permittivity, height=height)


courant = 0.5


def upper_gap(stacked, dimension):
    widths = [(0, 0)] * 4
    widths[dimension] = (0, 1)
    padded = jnp.pad(stacked, widths)
    ahead = lax.slice_in_dim(padded, 1, stacked.shape[dimension] + 1, axis=dimension)
    return ahead - stacked


def lower_gap(stacked, dimension):
    widths = [(0, 0)] * 4
    widths[dimension] = (1, 0)
    padded = jnp.pad(stacked, widths)
    behind = lax.slice_in_dim(padded, 0, stacked.shape[dimension], axis=dimension)
    return stacked - behind


def stacked_curl(stacked, upward):
    gap_fn = upper_gap if upward else lower_gap
    along_x = gap_fn(stacked[1:3], 3)
    along_y = gap_fn(jnp.stack([stacked[0], stacked[2]]), 2)
    along_z = gap_fn(stacked[0:2], 1)
    return jnp.stack([along_y[1] - along_z[1], along_z[0] - along_x[1], along_x[0] - along_y[0]])


def reference(forward_e, forward_h, adjoint_e, adjoint_h, material, inv_permittivity, height):
    coefficient = jnp.zeros(material.shape, jnp.float32)
    for number in range(MATERIALS):
        coefficient = coefficient + jnp.where(material == number, inv_permittivity[number], jnp.float32(0.0))
    dual_e = adjoint_e.astype(jnp.float32)
    dual_h = adjoint_h.astype(jnp.float32)
    stored = [dual_e]
    for number in range(STEPS):
        dual_h = dual_h + courant * stacked_curl(dual_e, True)
        dual_e = dual_e - (courant * coefficient) * stacked_curl(dual_h, False)
        if number + 1 < STEPS:
            stored.append(dual_e)
    field_e = forward_e.astype(jnp.float32)
    field_h = forward_h.astype(jnp.float32)
    summed = jnp.zeros(material.shape, jnp.float32)
    for number in range(STEPS):
        field_h = field_h - courant * stacked_curl(field_e, True)
        field_e = field_e + (courant * coefficient) * stacked_curl(field_h, False)
        partner = stored[STEPS - 1 - number]
        product = field_e[0] * partner[0] + field_e[1] * partner[1] + field_e[2] * partner[2]
        summed = summed + product
    depth_index = lax.broadcasted_iota(jnp.int32, material.shape, 0)
    texture = depth_index < height[None]
    column_grad = jnp.sum(jnp.where(texture, summed, jnp.float32(0.0)), axis=0)
    return column_grad, dual_h
```

```python
import functools

import jax
import jax.numpy as jnp
import numpy as np
from jax import lax
from jax.experimental import pallas as pl
from jax.experimental.pallas import tpu as pltpu
from jax.sharding import PartitionSpec as P

STEPS = 3
COURANT = 0.5
LANES = 128
TILE = 8
WIDE = 3
SHIFT = 4
COUNT = 13
FE, FH, AE, AH, KAPPA = 0, 3, 6, 9, 12
LOW_DEPTH = [3] * 3 + [3] * 3 + [2] * 3 + [2] * 3 + [2]
HIGH_DEPTH = [3] * 3 + [2] * 3 + [3] * 3 + [2] * 3 + [2]
LAYERS = sum(LOW_DEPTH)
SCALE = [1.0] * 3 + [-1.0 / COURANT] * 3 + [1.0] * 3 + [1.0 / COURANT] * 3 + [1.0]
F32 = jnp.float32
BF16 = jnp.bfloat16


def layers_to_next(length):
    return [(c, length - d + k, k - d) for c, d in enumerate(LOW_DEPTH) for k in range(d)]


def layers_to_previous(length):
    return [(c, k, length + k) for c, d in enumerate(HIGH_DEPTH) for k in range(d)]


def swap_pairs(length, offset):
    pairs = []
    for i in range(offset, length - 1, 2):
        pairs += [(i, i + 1), (i + 1, i)]
    return pairs


def swap(array, axis, offset):
    return lax.ppermute(array, axis, swap_pairs(lax.axis_size(axis), offset))


def row_picker(rows):
    to_next = np.zeros((LAYERS, COUNT * rows), np.float32)
    to_previous = np.zeros((LAYERS, COUNT * rows), np.float32)
    for n, (c, own, _) in enumerate(layers_to_next(rows)):
        to_next[n, c * rows + own] = 1
    for n, (c, own, _) in enumerate(layers_to_previous(rows)):
        to_previous[n, c * rows + own] = 1
    even = np.concatenate([to_next, to_previous])
    odd = np.concatenate([to_previous, to_next])
    return even, odd


def row_placer(rows):
    low = np.zeros((COUNT * TILE, LAYERS), np.float32)
    high = np.zeros((COUNT * TILE, LAYERS), np.float32)
    for n, (c, _, there) in enumerate(layers_to_next(rows)):
        low[c * TILE + there + SHIFT, n] = SCALE[c]
    for n, (c, _, there) in enumerate(layers_to_previous(rows)):
        high[c * TILE + there - rows + SHIFT, n] = SCALE[c]
    even = np.concatenate([high, low], axis=1)
    odd = np.concatenate([low, high], axis=1)
    return even, odd


def lane_of(shape):
    return lax.broadcasted_iota(jnp.int32, shape, len(shape) - 1)


def row_of(shape):
    return lax.broadcasted_iota(jnp.int32, shape, len(shape) - 2)


def own_field(refs, c, z):
    fe, fh, ae, ah, material = refs
    if c == KAPPA:
        return (material[z] + 1).astype(F32).astype(BF16)
    return (fe, fh, ae, ah)[c // 3][c % 3, z]


def pack_kernel(x_messages, flags, fe, fh, ae, ah, material, picker, *outs):
    depth, rows, cols = material.shape
    refs = (fe, fh, ae, ah, material)
    x_out = outs[:x_messages]
    z_out, ya_out, yb_out = outs[x_messages:]
    chunk = 8
    odd_x, odd_z = flags[0], flags[1]

    for number in range(x_messages):
        first = jnp.where(odd_x == number, 1, 0)
        offset = pl.multiple_of(first * (cols - LANES), LANES)
        row = row_of((LANES, LANES))
        lane = lane_of((LANES, LANES))
        spot = lane % TILE
        top = jnp.where(spot >= TILE - WIDE, LANES - TILE + spot, -1)
        bottom = jnp.where(spot < WIDE, spot, -1)
        picked = row == jnp.where(first == 1, top, bottom)
        pickers = [
            jnp.where(picked & (lane // TILE == c), 1.0, 0.0).astype(BF16) for c in range(COUNT)
        ]

        def columns(step, _):
            start = step * chunk
            total = jnp.zeros((chunk * rows, LANES), F32)
            for c in range(COUNT):
                if c == KAPPA:
                    part = material[pl.ds(start, chunk), :, pl.ds(offset, LANES)]
                    part = (part + 1).astype(F32).astype(BF16)
                else:
                    part = (fe, fh, ae, ah)[c // 3][
                        c % 3, pl.ds(start, chunk), :, pl.ds(offset, LANES)
                    ]
                total += jnp.dot(
                    part.reshape(chunk * rows, LANES), pickers[c], preferred_element_type=F32
                )
            x_out[number][pl.ds(start, chunk)] = total.reshape(chunk, rows, LANES)
            return 0

        lax.fori_loop(0, depth // chunk, columns, 0)

    @pl.when(odd_z == 0)
    def _():
        for n, (c, own, _) in enumerate(layers_to_next(depth)):
            z_out[n] = own_field(refs, c, own).astype(F32)

    @pl.when(odd_z == 1)
    def _():
        for n, (c, own, _) in enumerate(layers_to_previous(depth)):
            z_out[n] = own_field(refs, c, own).astype(F32)

    def plane(z, _):
        stacked = jnp.concatenate([own_field(refs, c, z) for c in range(COUNT)], axis=0)
        picked = jnp.dot(picker[...], stacked, preferred_element_type=F32)
        ya_out[z] = picked[:LAYERS]
        yb_out[z] = picked[LAYERS:]
        return 0

    lax.fori_loop(0, depth, plane, 0)


def edge_rows(array, odd, message):
    rows = array.shape[0]
    row = row_of((TILE, LANES))
    last = pltpu.roll(array[rows - TILE:], 4, 0)
    first = pltpu.roll(array[:TILE], 4, 0)
    last = jnp.where((row >= 1) & (row < 4), last, 0.0)
    first = jnp.where((row >= 4) & (row < 7), first, 0.0)
    return jnp.where(odd == message, last, first)


def corner_kernel(flags, xp, xz, zr, a_out, b_out):
    depth, rows, _ = xp.shape
    cols = zr.shape[2]
    tiles = cols // LANES
    odd_y, odd_z = flags[2], flags[1]
    base = LAYERS * tiles
    for message, out in ((0, a_out), (1, b_out)):
        for n in range(LAYERS):
            for t in range(tiles):
                out[n * tiles + t] = edge_rows(
                    zr[n, :, t * LANES:(t + 1) * LANES], odd_y, message
                )

        def plane(z, _):
            out[base + WIDE + z] = edge_rows(xp[z], odd_y, message)
            return 0

        lax.fori_loop(0, depth, plane, 0)
        there = jnp.where(odd_z == 1, 0, depth + WIDE)
        for k in range(WIDE):
            out[base + there + k] = edge_rows(xz[k], odd_y, message)
            out[base + depth + WIDE - there + k] = jnp.zeros((TILE, LANES), F32)


def spread(tiles, halo):
    low = row_of((TILE, LANES)) < SHIFT
    turned = [pltpu.roll(t, SHIFT, 0) for t in tiles]
    out = [jnp.where(low, halo, turned[0])]
    for before, after in zip(turned, turned[1:]):
        out.append(jnp.where(low, before, after))
    out.append(jnp.where(low, turned[-1], halo))
    return out


def gather(tiles):
    low = row_of((TILE, LANES)) < SHIFT
    turned = [pltpu.roll(t, SHIFT, 0) for t in tiles]
    return [jnp.where(low, before, after) for before, after in zip(turned, turned[1:])]


def window_kernel(
    flags, inverse, fe, fh, ae, ah, material, height, xp, xz, zr, ya, yb, corner_a, corner_b,
    placer, grad_out, dual_out, field, stored, wide_x,
):
    depth, rows, cols = material.shape
    own = cols // LANES
    tiles = own + 1
    blocks = rows // TILE + 1
    planes = depth + 2 * WIDE
    refs = (fe, fh, ae, ah, material)
    odd_z = flags[1]
    has_low, has_high = flags[5], flags[6]
    start_z = flags[7]
    row = row_of((TILE, LANES))
    lane = lane_of((TILE, LANES))

    def lane_tile(array, t):
        return array[:, t * LANES:(t + 1) * LANES]

    zero = jnp.zeros((TILE, LANES), F32)
    for t in range(tiles):
        for b in range(blocks):
            for c in range(3):
                field[FH + c, WIDE - 1, t, pl.ds(b * TILE, TILE)] = zero
                field[AH + c, WIDE - 1, t, pl.ds(b * TILE, TILE)] = zero
                field[FE + c, depth + WIDE, t, pl.ds(b * TILE, TILE)] = zero
                field[AE + c, depth + WIDE, t, pl.ds(b * TILE, TILE)] = zero
                stored[c, depth + WIDE, t, pl.ds(b * TILE, TILE)] = zero
                stored[3 + c, depth + WIDE, t, pl.ds(b * TILE, TILE)] = zero

    base = LAYERS * own

    def put_wide(slot, own_rows):
        halo = corner_a[base + slot] + corner_b[base + slot]
        parts = spread([own_rows[b * TILE:(b + 1) * TILE] for b in range(blocks - 1)], halo)
        for b, part in enumerate(parts):
            wide_x[slot, pl.ds(b * TILE, TILE)] = part

    def wide_plane(z, _):
        put_wide(z + WIDE, xp[z])
        return 0

    lax.fori_loop(0, depth, wide_plane, 0)
    there = jnp.where(odd_z == 1, 0, depth + WIDE)
    for k in range(WIDE):
        put_wide(there + k, xz[k])
        put_wide(depth + WIDE - there + k, jnp.zeros((rows, LANES), F32))

    def place_columns(c, _):
        scale = jnp.where(
            (c >= FH) & (c < FH + 3), SCALE[FH], jnp.where((c >= AH) & (c < AH + 3), SCALE[AH], 1.0)
        )
        source = row_of((LANES, LANES))
        target = lane_of((LANES, LANES))
        spot = source % TILE
        lands = jnp.where(spot < TILE // 2, spot, LANES - TILE + spot)
        placed = (target == lands) & (source // TILE == c)
        matrix = jnp.where(placed, scale, 0.0).astype(BF16)
        block = wide_x[...].reshape(planes * blocks * TILE, LANES).astype(BF16)
        result = jnp.dot(block, matrix, preferred_element_type=F32)
        field[c, :, own] = result.reshape(planes, blocks * TILE, LANES)
        return 0

    lax.fori_loop(0, COUNT, place_columns, 0)

    def put(c, slot, t, own_tiles, halo):
        for b, part in enumerate(spread(own_tiles, halo)):
            field[c, slot, t, pl.ds(b * TILE, TILE)] = part

    def halo_planes(layers):
        for n, (c, _, position) in enumerate(layers):
            for t in range(own):
                whole = lane_tile(zr[n], t)
                halo = corner_a[n * own + t] + corner_b[n * own + t]
                pieces = [whole[b * TILE:(b + 1) * TILE] for b in range(blocks - 1)]
                if SCALE[c] != 1.0:
                    pieces = [p * SCALE[c] for p in pieces]
                    halo = halo * SCALE[c]
                put(c, position + WIDE, t, pieces, halo)

    @pl.when(odd_z == 0)
    def _():
        halo_planes(layers_to_previous(depth))

    @pl.when(odd_z == 1)
    def _():
        halo_planes(layers_to_next(depth))

    def own_plane(z, _):
        arrived = jnp.concatenate([ya[z], yb[z]], axis=0).astype(BF16)
        halos = jnp.dot(placer[...], arrived, preferred_element_type=F32)
        for c in range(COUNT):
            whole = own_field(refs, c, z).astype(F32)
            for t in range(own):
                halo = lane_tile(halos[c * TILE:(c + 1) * TILE], t)
                part = lane_tile(whole, t)
                pieces = [part[b * TILE:(b + 1) * TILE] for b in range(blocks - 1)]
                if SCALE[c] != 1.0:
                    pieces = [p * SCALE[c] for p in pieces]
                put(c, z + WIDE, t, pieces, halo)
        return 0

    lax.fori_loop(0, depth, own_plane, 0)

    squared = [inverse[m] * (COURANT * COURANT) for m in range(inverse.shape[0])]

    def factor_plane(slot, _):
        for t in range(tiles):
            for b in range(blocks):
                at = (KAPPA, slot, t, pl.ds(b * TILE, TILE))
                number = field[at]
                value = jnp.zeros((TILE, LANES), F32)
                for m, weight in enumerate(squared):
                    value = jnp.where(number == m + 1, weight, value)
                field[at] = value
        return 0

    lax.fori_loop(1, planes - 1, factor_plane, 0)

    keep_row = jnp.where((row < SHIFT) & (flags[3] == 1), 0.0, 1.0)
    keep_lane = jnp.where((lane >= LANES // 2) & (flags[4] == 1), 0.0, 1.0)

    def mask(value, t, b):
        if b == 0:
            value = value * keep_row
        if t == own:
            value = value * keep_lane
        return value

    def ahead_rows(ref, c, slot, t, b, tile):
        if b == blocks - 1:
            return pltpu.roll(tile, TILE - 1, 0)
        return ref[c, slot, t, pl.ds(b * TILE + 1, TILE)]

    def behind_rows(ref, c, slot, t, b, tile):
        if b == 0:
            return pltpu.roll(tile, 1, 0)
        return ref[c, slot, t, pl.ds(b * TILE - 1, TILE)]

    def ahead_lanes(parts):
        turned = [pltpu.roll(p, LANES - 1, 1) for p in parts]
        return [jnp.where(lane == LANES - 1, turned[(t + 1) % tiles], turned[t]) for t in range(tiles)]

    def behind_lanes(parts):
        turned = [pltpu.roll(p, 1, 1) for p in parts]
        return [jnp.where(lane == 0, turned[(t - 1) % tiles], turned[t]) for t in range(tiles)]

    def span(low, high):
        return WIDE + jnp.where(has_low == 1, low, 0), WIDE + depth + jnp.where(has_high == 1, high, 0)

    def rows_at(b):
        return pl.ds(b * TILE, TILE)

    def magnetic(e, g, low, high, emit=None):
        e_ref, e0 = e
        g0 = g
        width = own if emit is not None else tiles

        def plane(slot, _):
            results = {}
            for b in range(blocks):
                at = rows_at(b)
                here = [[e_ref[e0 + c, slot, t, at] for t in range(tiles)] for c in range(3)]
                y_x = ahead_lanes(here[1])
                z_x = ahead_lanes(here[2])
                for t in range(width):
                    ex, ey, ez = here[0][t], here[1][t], here[2][t]
                    ex_y = ahead_rows(e_ref, e0, slot, t, b, ex)
                    ez_y = ahead_rows(e_ref, e0 + 2, slot, t, b, ez)
                    ex_z = e_ref[e0, slot + 1, t, at]
                    ey_z = e_ref[e0 + 1, slot + 1, t, at]
                    curl = (
                        (ez_y - ez) - (ey_z - ey),
                        (ex_z - ex) - (z_x[t] - ez),
                        (y_x[t] - ey) - (ex_y - ex),
                    )
                    for c in range(3):
                        value = field[g0 + c, slot, t, at] + curl[c]
                        if emit is None:
                            field[g0 + c, slot, t, at] = mask(value, t, b)
                        else:
                            results[c, t, b] = value
            if emit is not None:
                emit(slot, results)
            return 0

        begin, end = span(low, high)
        lax.fori_loop(begin, end, plane, 0)

    def electric(e, g, to, low, high, partner=None, totals=None):
        e_ref, e0 = e
        to_ref, to0 = to
        g0 = g

        def plane(slot, carry):
            carry = list(carry)
            if partner is not None:
                p_ref, p0 = partner
                position = slot - WIDE
                inside = (position >= 0) & (position < depth)
                position = jnp.where(inside, position + start_z, jnp.int32(2**30))
            for b in range(blocks):
                at = rows_at(b)
                here = [[field[g0 + c, slot, t, at] for t in range(tiles)] for c in range(3)]
                y_x = behind_lanes(here[1])
                z_x = behind_lanes(here[2])
                for t in range(tiles):
                    gx, gy, gz = here[0][t], here[1][t], here[2][t]
                    gx_y = behind_rows(field, g0, slot, t, b, gx)
                    gz_y = behind_rows(field, g0 + 2, slot, t, b, gz)
                    gx_z = field[g0, slot - 1, t, at]
                    gy_z = field[g0 + 1, slot - 1, t, at]
                    curl = (
                        (gz - gz_y) - (gy - gy_z),
                        (gx - gx_z) - (gz - z_x[t]),
                        (gy - y_x[t]) - (gx - gx_y),
                    )
                    factor = field[KAPPA, slot, t, at]
                    product = None
                    for c in range(3):
                        value = e_ref[e0 + c, slot, t, at] - factor * curl[c]
                        to_ref[to0 + c, slot, t, at] = value
                        if partner is not None and t < own:
                            term = value * p_ref[p0 + c, slot, t, at]
                            product = term if product is None else product + term
                    if product is not None:
                        inside = position < limits[t * blocks + b]
                        carry[t * blocks + b] += jnp.where(inside, product, 0.0)
            return tuple(carry)

        begin, end = span(low, high)
        return lax.fori_loop(begin, end, plane, totals if totals is not None else ())

    first = (field, AE)
    second = (stored, 0)
    third = (stored, 3)
    forward = (field, FE)

    def emit_dual(slot, results):
        for c in range(3):
            for t in range(own):
                values = gather([results[c, t, b] for b in range(blocks)])
                for b, value in enumerate(values):
                    dual_out[c, slot - WIDE, rows_at(b), t * LANES:(t + 1) * LANES] = value * COURANT

    magnetic(first, AH, -2, 2)
    electric(first, AH, second, -1, 2)
    magnetic(second, AH, -1, 1)
    electric(second, AH, third, 0, 1)
    magnetic(third, AH, 0, 0, emit_dual)

    none = jnp.zeros((TILE, LANES), jnp.int32)
    limits = []
    for t in range(own):
        part = lane_tile(height[...], t)
        limits += spread([part[b * TILE:(b + 1) * TILE] for b in range(blocks - 1)], none)
    totals = (zero,) * (own * blocks)
    magnetic(forward, FH, -3, 2)
    totals = electric(forward, FH, forward, -2, 2, third, totals)
    magnetic(forward, FH, -2, 1)
    totals = electric(forward, FH, forward, -1, 1, second, totals)
    magnetic(forward, FH, -1, 0)
    totals = electric(forward, FH, forward, 0, 0, first, totals)
    for t in range(own):
        values = gather(list(totals[t * blocks:(t + 1) * blocks]))
        for b, value in enumerate(values):
            grad_out[rows_at(b), t * LANES:(t + 1) * LANES] = value


def local(forward_e, forward_h, adjoint_e, adjoint_h, material, inv_permittivity, height):
    depth, rows, cols = material.shape
    tiles = cols // LANES
    gx, gy, gz = (lax.axis_index(a) for a in ("gx", "gy", "gz"))
    nx, ny, nz = (lax.axis_size(a) for a in ("gx", "gy", "gz"))
    assert nz == 2
    flags = jnp.stack([
        gx % 2, gz % 2, gy % 2,
        jnp.where(gy == 0, 1, 0), jnp.where(gx == 0, 1, 0),
        jnp.where(gz > 0, 1, 0), jnp.where(gz < nz - 1, 1, 0),
        gz * depth,
    ]).astype(jnp.int32)
    picker = [jnp.asarray(m, BF16) for m in row_picker(rows)]
    picker = jnp.where(gy % 2 == 0, picker[0], picker[1])
    placer = [jnp.asarray(m, BF16) for m in row_placer(rows)]
    placer = jnp.where(gy % 2 == 0, placer[0], placer[1])
    vmem = pl.BlockSpec(memory_space=pltpu.VMEM)
    smem = pl.BlockSpec(memory_space=pltpu.SMEM)
    params = pltpu.CompilerParams(vmem_limit_bytes=60 * 1024 * 1024)
    x_messages = 1 if nx == 2 else 2

    y_shape = jax.ShapeDtypeStruct((depth, LAYERS, cols), F32)
    packed = pl.pallas_call(
        functools.partial(pack_kernel, x_messages),
        out_shape=[jax.ShapeDtypeStruct((depth, rows, LANES), F32)] * x_messages
        + [jax.ShapeDtypeStruct((LAYERS, rows, cols), F32), y_shape, y_shape],
        in_specs=[smem] + [vmem] * 6,
        out_specs=[vmem] * (x_messages + 3),
        compiler_params=params,
        name="pack",
    )(flags, forward_e, forward_h, adjoint_e, adjoint_h, material, picker)
    z_message, ya, yb = packed[x_messages:]
    yb = swap(yb, "gy", 1)
    ya = swap(ya, "gy", 0)
    xp = swap(packed[0], "gx", 0)
    if x_messages == 2:
        xp = xp + swap(packed[1], "gx", 1)
    zr = swap(z_message, "gz", 0)
    xz = lax.dynamic_slice_in_dim(xp, jnp.where(gz % 2 == 0, depth - WIDE, 0), WIDE, axis=0)
    xz = swap(xz, "gz", 0)

    corner_shape = jax.ShapeDtypeStruct((LAYERS * tiles + depth + 2 * WIDE, TILE, LANES), F32)
    corner_a, corner_b = pl.pallas_call(
        corner_kernel,
        out_shape=[corner_shape, corner_shape],
        in_specs=[smem] + [vmem] * 3,
        out_specs=[vmem] * 2,
        compiler_params=params,
        name="corners",
    )(flags, xp, xz, zr)
    corner_b = swap(corner_b, "gy", 1)
    corner_a = swap(corner_a, "gy", 0)

    blocks = rows // TILE + 1
    planes = depth + 2 * WIDE
    block = (planes, tiles + 1, blocks * TILE, LANES)
    grad, dual = pl.pallas_call(
        window_kernel,
        out_shape=[
            jax.ShapeDtypeStruct((rows, cols), F32),
            jax.ShapeDtypeStruct((3, depth, rows, cols), F32),
        ],
        in_specs=[smem, smem] + [vmem] * 14,
        out_specs=[vmem] * 2,
        scratch_shapes=[
            pltpu.VMEM((COUNT,) + block, F32),
            pltpu.VMEM((6,) + block, F32),
            pltpu.VMEM((planes, blocks * TILE, LANES), F32),
        ],
        compiler_params=params,
        name="window",
    )(
        flags, inv_permittivity, forward_e, forward_h, adjoint_e, adjoint_h, material, height,
        xp, xz, zr, ya, yb, corner_a, corner_b, placer,
    )
    return grad + swap(grad, "gz", 0), dual


def solution(mesh):
    fields = P(None, "gz", "gy", "gx")
    return jax.shard_map(
        local,
        mesh=mesh,
        in_specs=(fields, fields, fields, fields, P("gz", "gy", "gx"), P(), P("gy", "gx")),
        out_specs=(P("gy", "gx"), fields),
        check_vma=False,
    )
```

```python
import functools

import jax
import jax.numpy as jnp
import numpy as np
from jax import lax
from jax.experimental import pallas as pl
from jax.experimental.pallas import tpu as pltpu
from jax.sharding import PartitionSpec as P

STEPS = 3
COURANT = 0.5
LANES = 128
TILE = 8
WIDE = 3
BEFORE = 4
AFTER = 5
UNROLL = 2
SHIFT = 4
COUNT = 13
FE, FH, AE, AH, KAPPA = 0, 3, 6, 9, 12
LOW_DEPTH = [3] * 3 + [3] * 3 + [2] * 3 + [2] * 3 + [2]
HIGH_DEPTH = [3] * 3 + [2] * 3 + [3] * 3 + [2] * 3 + [2]
LAYERS = sum(LOW_DEPTH)
SCALE = [1.0] * 3 + [-1.0 / COURANT] * 3 + [1.0] * 3 + [1.0 / COURANT] * 3 + [1.0]
F32 = jnp.float32
BF16 = jnp.bfloat16


def layers_to_next(length):
    return [(c, length - d + k, k - d) for c, d in enumerate(LOW_DEPTH) for k in range(d)]


def layers_to_previous(length):
    return [(c, k, length + k) for c, d in enumerate(HIGH_DEPTH) for k in range(d)]


def swap_pairs(length, offset):
    pairs = []
    for i in range(offset, length - 1, 2):
        pairs += [(i, i + 1), (i + 1, i)]
    return pairs


def swap(array, axis, offset):
    return lax.ppermute(array, axis, swap_pairs(lax.axis_size(axis), offset))


def row_picker(rows):
    to_next = np.zeros((LAYERS, COUNT * rows), np.float32)
    to_previous = np.zeros((LAYERS, COUNT * rows), np.float32)
    for n, (c, own, _) in enumerate(layers_to_next(rows)):
        to_next[n, c * rows + own] = 1
    for n, (c, own, _) in enumerate(layers_to_previous(rows)):
        to_previous[n, c * rows + own] = 1
    even = np.concatenate([to_next, to_previous])
    odd = np.concatenate([to_previous, to_next])
    return even, odd


def row_placer(rows):
    low = np.zeros((COUNT * TILE, LAYERS), np.float32)
    high = np.zeros((COUNT * TILE, LAYERS), np.float32)
    for n, (c, _, there) in enumerate(layers_to_next(rows)):
        low[c * TILE + there + SHIFT, n] = SCALE[c]
    for n, (c, _, there) in enumerate(layers_to_previous(rows)):
        high[c * TILE + there - rows + SHIFT, n] = SCALE[c]
    even = np.concatenate([high, low], axis=1)
    odd = np.concatenate([low, high], axis=1)
    return even, odd


def lane_of(shape):
    return lax.broadcasted_iota(jnp.int32, shape, len(shape) - 1)


def row_of(shape):
    return lax.broadcasted_iota(jnp.int32, shape, len(shape) - 2)


def own_field(refs, c, z):
    fe, fh, ae, ah, material = refs
    if c == KAPPA:
        return (material[z] + 1).astype(F32).astype(BF16)
    return (fe, fh, ae, ah)[c // 3][c % 3, z]


def pack_kernel(x_messages, flags, fe, fh, ae, ah, material, picker, *outs):
    depth, rows, cols = material.shape
    refs = (fe, fh, ae, ah, material)
    x_out = outs[:x_messages]
    z_out, ya_out, yb_out = outs[x_messages:]
    chunk = 8
    odd_x, odd_z = flags[0], flags[1]

    for number in range(x_messages):
        first = jnp.where(odd_x == number, 1, 0)
        offset = pl.multiple_of(first * (cols - LANES), LANES)
        row = row_of((LANES, LANES))
        lane = lane_of((LANES, LANES))
        spot = lane % TILE
        top = jnp.where(spot >= TILE - WIDE, LANES - TILE + spot, -1)
        bottom = jnp.where(spot < WIDE, spot, -1)
        picked = row == jnp.where(first == 1, top, bottom)
        pickers = [
            jnp.where(picked & (lane // TILE == c), 1.0, 0.0).astype(BF16) for c in range(COUNT)
        ]

        def columns(step, _):
            start = step * chunk
            total = jnp.zeros((chunk * rows, LANES), F32)
            for c in range(COUNT):
                if c == KAPPA:
                    part = material[pl.ds(start, chunk), :, pl.ds(offset, LANES)]
                    part = (part + 1).astype(F32).astype(BF16)
                else:
                    part = (fe, fh, ae, ah)[c // 3][
                        c % 3, pl.ds(start, chunk), :, pl.ds(offset, LANES)
                    ]
                total += jnp.dot(
                    part.reshape(chunk * rows, LANES), pickers[c], preferred_element_type=F32
                )
            x_out[number][pl.ds(start, chunk)] = total.reshape(chunk, rows, LANES)
            return 0

        lax.fori_loop(0, depth // chunk, columns, 0)

    @pl.when(odd_z == 0)
    def _():
        for n, (c, own, _) in enumerate(layers_to_next(depth)):
            z_out[n] = own_field(refs, c, own).astype(F32)

    @pl.when(odd_z == 1)
    def _():
        for n, (c, own, _) in enumerate(layers_to_previous(depth)):
            z_out[n] = own_field(refs, c, own).astype(F32)

    def plane(z, _):
        stacked = jnp.concatenate([own_field(refs, c, z) for c in range(COUNT)], axis=0)
        picked = jnp.dot(picker[...], stacked, preferred_element_type=F32)
        ya_out[z] = picked[:LAYERS]
        yb_out[z] = picked[LAYERS:]
        return 0

    lax.fori_loop(0, depth, plane, 0)


def edge_rows(array, odd, message):
    rows = array.shape[0]
    row = row_of((TILE, LANES))
    last = pltpu.roll(array[rows - TILE:], 4, 0)
    first = pltpu.roll(array[:TILE], 4, 0)
    last = jnp.where((row >= 1) & (row < 4), last, 0.0)
    first = jnp.where((row >= 4) & (row < 7), first, 0.0)
    return jnp.where(odd == message, last, first)


def corner_kernel(flags, xp, xz, zr, a_out, b_out):
    depth, rows, _ = xp.shape
    cols = zr.shape[2]
    tiles = cols // LANES
    odd_y, odd_z = flags[2], flags[1]
    base = LAYERS * tiles
    for message, out in ((0, a_out), (1, b_out)):
        for n in range(LAYERS):
            for t in range(tiles):
                out[n * tiles + t] = edge_rows(
                    zr[n, :, t * LANES:(t + 1) * LANES], odd_y, message
                )

        def plane(z, _):
            out[base + WIDE + z] = edge_rows(xp[z], odd_y, message)
            return 0

        lax.fori_loop(0, depth, plane, 0)
        there = jnp.where(odd_z == 1, 0, depth + WIDE)
        for k in range(WIDE):
            out[base + there + k] = edge_rows(xz[k], odd_y, message)
            out[base + depth + WIDE - there + k] = jnp.zeros((TILE, LANES), F32)


def spread(tiles, halo):
    low = row_of((TILE, LANES)) < SHIFT
    turned = [pltpu.roll(t, SHIFT, 0) for t in tiles]
    out = [jnp.where(low, halo, turned[0])]
    for before, after in zip(turned, turned[1:]):
        out.append(jnp.where(low, before, after))
    out.append(jnp.where(low, turned[-1], halo))
    return out


def gather(tiles):
    low = row_of((TILE, LANES)) < SHIFT
    turned = [pltpu.roll(t, SHIFT, 0) for t in tiles]
    return [jnp.where(low, before, after) for before, after in zip(turned, turned[1:])]


def window_kernel(
    flags, inverse, fe, fh, ae, ah, material, height, xp, xz, zr, ya, yb, corner_a, corner_b,
    placer, grad_out, dual_out, forward_e, forward_g, dual_e, dual_g, second_e, third_e, factor,
    wide_x,
):
    depth, rows, cols = material.shape
    own = cols // LANES
    tiles = own + 1
    blocks = rows // TILE + 1
    planes = depth + 2 * WIDE
    refs = (fe, fh, ae, ah, material)
    odd_z = flags[1]
    start_z = flags[7]
    row = row_of((TILE, LANES))
    lane = lane_of((TILE, LANES))
    zero = jnp.zeros((TILE, LANES), F32)
    squared = [inverse[m] * (COURANT * COURANT) for m in range(inverse.shape[0])]

    def rows_at(b):
        return pl.ds(b * TILE, TILE)

    def lane_tile(array, t):
        return array[:, t * LANES:(t + 1) * LANES]

    def row_tiles(array):
        return [array[b * TILE:(b + 1) * TILE] for b in range(blocks - 1)]

    def target(c):
        if c == KAPPA:
            return factor, 0
        return (forward_e, forward_g, dual_e, dual_g)[c // 3], c % 3

    def weight(number):
        value = jnp.zeros(number.shape, F32)
        for m, w in enumerate(squared):
            value = jnp.where(number == m + 1, w, value)
        return value

    for t in range(tiles):
        for b in range(blocks):
            for c in range(3):
                forward_g[c, BEFORE - 1, t, rows_at(b)] = zero
                dual_g[c, BEFORE - 1, t, rows_at(b)] = zero
                for ref in (forward_e, dual_e, second_e, third_e):
                    ref[c, depth + BEFORE, t, rows_at(b)] = zero

    base = LAYERS * own

    def put_wide(slot, own_rows):
        halo = corner_a[base + slot] + corner_b[base + slot]
        return slot, spread(row_tiles(own_rows), halo)

    def store_wide(items):
        for slot, parts in items:
            for b, part in enumerate(parts):
                wide_x[slot, rows_at(b)] = part

    def wide_planes(step, _):
        store_wide([put_wide(step * 8 + k + WIDE, xp[step * 8 + k]) for k in range(8)])
        return 0

    lax.fori_loop(0, depth // 8, wide_planes, 0)
    there = jnp.where(odd_z == 1, 0, depth + WIDE)
    items = []
    for k in range(WIDE):
        items.append(put_wide(there + k, xz[k]))
        items.append(put_wide(depth + WIDE - there + k, jnp.zeros((rows, LANES), F32)))
    store_wide(items)

    source = row_of((LANES, LANES))
    spot = source % TILE
    lands = jnp.where(spot < TILE // 2, spot, LANES - TILE + spot) == lane_of((LANES, LANES))
    wide = wide_x[...].reshape(planes * blocks * TILE, LANES).astype(BF16)
    pairs = [(c, c + 1) if c + 1 < COUNT else (c,) for c in range(0, COUNT, 2)]
    for pair in pairs:
        matrix = [jnp.where(lands & (source // TILE == c), SCALE[c], 0.0).astype(BF16) for c in pair]
        matrix = jnp.concatenate(matrix, axis=1) if len(pair) > 1 else matrix[0]
        result = jnp.dot(wide, matrix, preferred_element_type=F32)
        for n, c in enumerate(pair):
            ref, at = target(c)
            value = lane_tile(result, n).reshape(planes, blocks * TILE, LANES)
            ref[at, pl.ds(BEFORE - WIDE, planes), own] = weight(value) if c == KAPPA else value

    def store(items):
        for c, slot, t, parts in items:
            ref, at = target(c)
            for b, part in enumerate(parts):
                ref[at, slot, t, rows_at(b)] = part

    def arrange(c, own_tiles, halo):
        if c == KAPPA:
            own_tiles = [weight(p) for p in own_tiles]
            halo = weight(halo)
        elif SCALE[c] != 1.0:
            own_tiles = [p * SCALE[c] for p in own_tiles]
        return spread(own_tiles, halo)

    def halo_planes(layers):
        for n, (c, _, position) in enumerate(layers):
            items = []
            for t in range(own):
                halo = (corner_a[n * own + t] + corner_b[n * own + t]) * SCALE[c]
                parts = arrange(c, row_tiles(lane_tile(zr[n], t)), halo)
                items.append((c, position + BEFORE, t, parts))
            store(items)

    @pl.when(odd_z == 0)
    def _():
        halo_planes(layers_to_previous(depth))

    @pl.when(odd_z == 1)
    def _():
        halo_planes(layers_to_next(depth))

    def own_planes(step, _):
        items = []
        for k in range(2):
            z = step * 2 + k
            arrived = jnp.concatenate([ya[z], yb[z]], axis=0).astype(BF16)
            halos = jnp.dot(placer[...], arrived, preferred_element_type=F32)
            for c in range(COUNT):
                whole = own_field(refs, c, z).astype(F32)
                for t in range(own):
                    halo = lane_tile(halos[c * TILE:(c + 1) * TILE], t)
                    parts = arrange(c, row_tiles(lane_tile(whole, t)), halo)
                    items.append((c, z + BEFORE, t, parts))
        store(items)
        return 0

    lax.fori_loop(0, depth // 2, own_planes, 0)

    keep_row = jnp.where((row < SHIFT) & (flags[3] == 1), 0.0, 1.0)
    keep_lane = jnp.where((lane >= LANES // 2) & (flags[4] == 1), 0.0, 1.0)

    def mask(value, t, b):
        if b == 0:
            value = value * keep_row
        if t == own:
            value = value * keep_lane
        return value

    def ahead_lanes(parts):
        turned = [pltpu.roll(p, LANES - 1, 1) for p in parts]
        return [jnp.where(lane == LANES - 1, turned[(t + 1) % tiles], turned[t]) for t in range(tiles)]

    def behind_lanes(parts):
        turned = [pltpu.roll(p, 1, 1) for p in parts]
        return [jnp.where(lane == 0, turned[(t - 1) % tiles], turned[t]) for t in range(tiles)]

    def reader(ref, slot):
        seen = {}

        def read(c, ahead, t, b):
            if (c, ahead, t, b) not in seen:
                seen[c, ahead, t, b] = ref[c, slot + ahead, t, rows_at(b)]
            return seen[c, ahead, t, b]

        def ahead_rows(c, ahead, t, b):
            if b == blocks - 1:
                return pltpu.roll(read(c, ahead, t, b), TILE - 1, 0)
            return ref[c, slot + ahead, t, pl.ds(b * TILE + 1, TILE)]

        def behind_rows(c, ahead, t, b):
            if b == 0:
                return pltpu.roll(read(c, ahead, t, b), 1, 0)
            return ref[c, slot + ahead, t, pl.ds(b * TILE - 1, TILE)]

        return read, ahead_rows, behind_rows

    def begin(count):
        return BEFORE + jnp.where(odd_z == 1, depth - count, 0)

    def magnetic(e, g, count, emit=None):
        width = own if emit is not None else tiles
        first = begin(count)

        def step(number, _):
            slot = first + number * UNROLL
            read, ahead_rows, _ = reader(e, slot)
            old, _, _ = reader(g, slot)
            results = {}
            for k in range(UNROLL):
                for b in range(blocks):
                    y_x = ahead_lanes([read(1, k, t, b) for t in range(tiles)])
                    z_x = ahead_lanes([read(2, k, t, b) for t in range(tiles)])
                    for t in range(width):
                        ex, ey, ez = (read(c, k, t, b) for c in range(3))
                        curl = (
                            (ahead_rows(2, k, t, b) - ez) - (read(1, k + 1, t, b) - ey),
                            (read(0, k + 1, t, b) - ex) - (z_x[t] - ez),
                            (y_x[t] - ey) - (ahead_rows(0, k, t, b) - ex),
                        )
                        for c in range(3):
                            value = old(c, k, t, b) + curl[c]
                            results[c, k, t, b] = value if emit is not None else mask(value, t, b)
            if emit is not None:
                emit(slot, results)
            else:
                for (c, k, t, b), value in results.items():
                    g[c, slot + k, t, rows_at(b)] = value
            return 0

        lax.fori_loop(0, count // UNROLL, step, 0)

    def electric(e, g, to, count, partner=None, totals=()):
        first = begin(count)

        def step(number, carry):
            carry = list(carry)
            slot = first + number * UNROLL
            read, _, behind_rows = reader(g, slot)
            old, _, _ = reader(e, slot)
            weights, _, _ = reader(factor, slot)
            results = {}
            for k in range(UNROLL):
                if partner is not None:
                    position = slot + k - BEFORE
                    inside = (position >= 0) & (position < depth)
                    position = jnp.where(inside, position + start_z, jnp.int32(2**30))
                for b in range(blocks):
                    y_x = behind_lanes([read(1, k, t, b) for t in range(tiles)])
                    z_x = behind_lanes([read(2, k, t, b) for t in range(tiles)])
                    for t in range(tiles):
                        gx, gy, gz = (read(c, k, t, b) for c in range(3))
                        curl = (
                            (gz - behind_rows(2, k, t, b)) - (gy - read(1, k - 1, t, b)),
                            (gx - read(0, k - 1, t, b)) - (gz - z_x[t]),
                            (gy - y_x[t]) - (gx - behind_rows(0, k, t, b)),
                        )
                        scale = weights(0, k, t, b)
                        product = None
                        for c in range(3):
                            value = old(c, k, t, b) - scale * curl[c]
                            results[c, k, t, b] = value
                            if partner is not None and t < own:
                                term = value * partner[c, slot + k, t, rows_at(b)]
                                product = term if product is None else product + term
                        if product is not None:
                            chosen = position < limits[t * blocks + b]
                            carry[t * blocks + b] += jnp.where(chosen, product, 0.0)
            for (c, k, t, b), value in results.items():
                to[c, slot + k, t, rows_at(b)] = value
            return tuple(carry)

        return lax.fori_loop(0, count // UNROLL, step, totals)

    def emit_dual(slot, results):
        for k in range(UNROLL):
            for c in range(3):
                for t in range(own):
                    values = gather([results[c, k, t, b] for b in range(blocks)])
                    for b, value in enumerate(values):
                        where = (c, slot + k - BEFORE, rows_at(b), pl.ds(t * LANES, LANES))
                        dual_out[where] = value * COURANT

    def count(low, high):
        return -(-(depth + max(low, high)) // UNROLL) * UNROLL

    magnetic(dual_e, dual_g, count(2, 2))
    electric(dual_e, dual_g, second_e, count(1, 2))
    magnetic(second_e, dual_g, count(1, 1))
    electric(second_e, dual_g, third_e, count(0, 1))
    magnetic(third_e, dual_g, depth, emit_dual)

    none = jnp.zeros((TILE, LANES), jnp.int32)
    limits = []
    for t in range(own):
        limits += spread(row_tiles(lane_tile(height[...], t)), none)
    totals = (zero,) * (own * blocks)
    magnetic(forward_e, forward_g, count(3, 2))
    totals = electric(forward_e, forward_g, forward_e, count(2, 2), third_e, totals)
    magnetic(forward_e, forward_g, count(2, 1))
    totals = electric(forward_e, forward_g, forward_e, count(1, 1), second_e, totals)
    magnetic(forward_e, forward_g, count(1, 0))
    totals = electric(forward_e, forward_g, forward_e, depth, dual_e, totals)
    for t in range(own):
        values = gather(list(totals[t * blocks:(t + 1) * blocks]))
        for b, value in enumerate(values):
            grad_out[rows_at(b), t * LANES:(t + 1) * LANES] = value


def local(forward_e, forward_h, adjoint_e, adjoint_h, material, inv_permittivity, height):
    depth, rows, cols = material.shape
    tiles = cols // LANES
    gx, gy, gz = (lax.axis_index(a) for a in ("gx", "gy", "gz"))
    nx, ny, nz = (lax.axis_size(a) for a in ("gx", "gy", "gz"))
    assert nz == 2
    flags = jnp.stack([
        gx % 2, gz % 2, gy % 2,
        jnp.where(gy == 0, 1, 0), jnp.where(gx == 0, 1, 0),
        jnp.where(gz > 0, 1, 0), jnp.where(gz < nz - 1, 1, 0),
        gz * depth,
    ]).astype(jnp.int32)
    picker = [jnp.asarray(m, BF16) for m in row_picker(rows)]
    picker = jnp.where(gy % 2 == 0, picker[0], picker[1])
    placer = [jnp.asarray(m, BF16) for m in row_placer(rows)]
    placer = jnp.where(gy % 2 == 0, placer[0], placer[1])
    vmem = pl.BlockSpec(memory_space=pltpu.VMEM)
    smem = pl.BlockSpec(memory_space=pltpu.SMEM)
    params = pltpu.CompilerParams(vmem_limit_bytes=60 * 1024 * 1024)
    x_messages = 1 if nx == 2 else 2

    y_shape = jax.ShapeDtypeStruct((depth, LAYERS, cols), F32)
    packed = pl.pallas_call(
        functools.partial(pack_kernel, x_messages),
        out_shape=[jax.ShapeDtypeStruct((depth, rows, LANES), F32)] * x_messages
        + [jax.ShapeDtypeStruct((LAYERS, rows, cols), F32), y_shape, y_shape],
        in_specs=[smem] + [vmem] * 6,
        out_specs=[vmem] * (x_messages + 3),
        compiler_params=params,
        name="pack",
    )(flags, forward_e, forward_h, adjoint_e, adjoint_h, material, picker)
    z_message, ya, yb = packed[x_messages:]
    yb = swap(yb, "gy", 1)
    ya = swap(ya, "gy", 0)
    xp = swap(packed[0], "gx", 0)
    if x_messages == 2:
        xp = xp + swap(packed[1], "gx", 1)
    zr = swap(z_message, "gz", 0)
    xz = lax.dynamic_slice_in_dim(xp, jnp.where(gz % 2 == 0, depth - WIDE, 0), WIDE, axis=0)
    xz = swap(xz, "gz", 0)

    corner_shape = jax.ShapeDtypeStruct((LAYERS * tiles + depth + 2 * WIDE, TILE, LANES), F32)
    corner_a, corner_b = pl.pallas_call(
        corner_kernel,
        out_shape=[corner_shape, corner_shape],
        in_specs=[smem] + [vmem] * 3,
        out_specs=[vmem] * 2,
        compiler_params=params,
        name="corners",
    )(flags, xp, xz, zr)
    corner_b = swap(corner_b, "gy", 1)
    corner_a = swap(corner_a, "gy", 0)

    blocks = rows // TILE + 1
    planes = depth + 2 * WIDE
    block = (BEFORE + depth + AFTER, tiles + 1, blocks * TILE, LANES)
    grad, dual = pl.pallas_call(
        window_kernel,
        out_shape=[
            jax.ShapeDtypeStruct((rows, cols), F32),
            jax.ShapeDtypeStruct((3, depth, rows, cols), F32),
        ],
        in_specs=[smem, smem] + [vmem] * 14,
        out_specs=[vmem] * 2,
        scratch_shapes=[
            *[pltpu.VMEM((3,) + block, F32)] * 6,
            pltpu.VMEM((1,) + block, F32),
            pltpu.VMEM((planes, blocks * TILE, LANES), F32),
        ],
        compiler_params=params,
        name="window",
    )(
        flags, inv_permittivity, forward_e, forward_h, adjoint_e, adjoint_h, material, height,
        xp, xz, zr, ya, yb, corner_a, corner_b, placer,
    )
    return grad + swap(grad, "gz", 0), dual


def solution(mesh):
    fields = P(None, "gz", "gy", "gx")
    return jax.shard_map(
        local,
        mesh=mesh,
        in_specs=(fields, fields, fields, fields, P("gz", "gy", "gx"), P(), P("gy", "gx")),
        out_specs=(P("gy", "gx"), fields),
        check_vma=False,
    )
```

```python
import functools

import jax
import jax.numpy as jnp
import numpy as np
from jax import lax
from jax.experimental import pallas as pl
from jax.experimental.pallas import tpu as pltpu
from jax.sharding import PartitionSpec as P

STEPS = 3
COURANT = 0.5
LANES = 128
TILE = 8
WIDE = 3
BEFORE = 5
AFTER = 5
UNROLL = 4
SHIFT = 4
COUNT = 13
FE, FH, AE, AH, KAPPA = 0, 3, 6, 9, 12
LOW_DEPTH = [3] * 3 + [3] * 3 + [2] * 3 + [2] * 3 + [2]
HIGH_DEPTH = [3] * 3 + [2] * 3 + [3] * 3 + [2] * 3 + [2]
LAYERS = sum(LOW_DEPTH)
SCALE = [1.0] * 3 + [-1.0 / COURANT] * 3 + [1.0] * 3 + [1.0 / COURANT] * 3 + [1.0]
F32 = jnp.float32
BF16 = jnp.bfloat16


def layers_to_next(length):
    return [(c, length - d + k, k - d) for c, d in enumerate(LOW_DEPTH) for k in range(d)]


def layers_to_previous(length):
    return [(c, k, length + k) for c, d in enumerate(HIGH_DEPTH) for k in range(d)]


def swap_pairs(length, offset):
    pairs = []
    for i in range(offset, length - 1, 2):
        pairs += [(i, i + 1), (i + 1, i)]
    return pairs


def swap(array, axis, offset):
    return lax.ppermute(array, axis, swap_pairs(lax.axis_size(axis), offset))


def two_ways(rows_in, to_next, to_previous):
    first, second = np.zeros((2, len(to_next), rows_in), np.float32)
    for n, index in enumerate(to_next):
        first[n, index] = 1
    for n, index in enumerate(to_previous):
        second[n, index] = 1
    return np.stack([np.concatenate([first, second]), np.concatenate([second, first])])


def row_picker(rows):
    return two_ways(
        COUNT * rows,
        [c * rows + own for c, own, _ in layers_to_next(rows)],
        [c * rows + own for c, own, _ in layers_to_previous(rows)],
    )


def corner_picker(rows):
    return two_ways(
        LAYERS * rows,
        [n * rows + rows - WIDE + k for n in range(LAYERS) for k in range(WIDE)],
        [n * rows + k for n in range(LAYERS) for k in range(WIDE)],
    )


def ways_back(rows_out, low, high):
    first = np.zeros((rows_out, len(low)), np.float32)
    second = np.zeros((rows_out, len(high)), np.float32)
    for n, (index, value) in enumerate(low):
        first[index, n] = value
    for n, (index, value) in enumerate(high):
        second[index, n] = value
    return np.stack([np.concatenate([second, first], 1), np.concatenate([first, second], 1)])


def row_placer(rows):
    low = [(c * TILE + there + SHIFT, SCALE[c]) for c, _, there in layers_to_next(rows)]
    high = [(c * TILE + there - rows + SHIFT, SCALE[c]) for c, _, there in layers_to_previous(rows)]
    return ways_back(COUNT * TILE, low, high)


def corner_placer():
    low = [(n * TILE + SHIFT - WIDE + k, 1) for n in range(LAYERS) for k in range(WIDE)]
    high = [(n * TILE + SHIFT + k, 1) for n in range(LAYERS) for k in range(WIDE)]
    return ways_back(LAYERS * TILE, low, high)


def column_table(depth):
    groups = depth // TILE
    assert groups * LAYERS <= LANES
    table = np.full((2, TILE, LANES), -1, np.int32)
    for way, layers in enumerate((layers_to_next(LANES), layers_to_previous(0))):
        for g in range(groups):
            for n, (c, own, there) in enumerate(layers):
                lane = g * LAYERS + n
                table[way, :4, lane] = c, own, there % LANES, g
    return table


def lane_of(shape):
    return lax.broadcasted_iota(jnp.int32, shape, len(shape) - 1)


def row_of(shape):
    return lax.broadcasted_iota(jnp.int32, shape, len(shape) - 2)


def own_field(refs, c, z):
    fe, fh, ae, ah, material = refs
    if c == KAPPA:
        return (material[z] + 1).astype(F32).astype(BF16)
    return (fe, fh, ae, ah)[c // 3][c % 3, z]


def place_on(axis):
    return lax.axis_index(axis), lax.rem(lax.axis_index(axis), 2)


def pack_kernel(x_messages, fe, fh, ae, ah, material, picker, table, *outs):
    chunk, rows, cols = material.shape
    refs = (fe, fh, ae, ah, material)
    x_out = outs[:x_messages]
    z_out, ya_out, yb_out = outs[x_messages:]
    odd_x, odd_y, odd_z = (place_on(axis)[1] for axis in ("gx", "gy", "gz"))
    step = pl.program_id(0)

    picked = [
        jnp.dot(
            picker[odd_y],
            jnp.concatenate([own_field(refs, c, z) for c in range(COUNT)], axis=0),
            preferred_element_type=F32,
        )
        for z in range(chunk)
    ]
    for z in range(chunk):
        ya_out[z] = picked[z][:LAYERS]
        yb_out[z] = picked[z][LAYERS:]

    for number, out in enumerate(x_out):
        way = odd_x ^ number
        offset = pl.multiple_of((1 - way) * (cols - LANES), LANES)
        total = jnp.zeros((chunk * rows, LANES), F32)
        of_field, of_lane, of_group = (table[way, k:k + 1, :] for k in (0, 1, 3))
        chosen = (row_of((LANES, LANES)) == of_lane) & (of_group == step)
        for c in range(COUNT):
            if c == KAPPA:
                part = material[:, :, pl.ds(offset, LANES)]
                part = (part + 1).astype(F32).astype(BF16)
            else:
                part = (fe, fh, ae, ah)[c // 3][c % 3, :, :, pl.ds(offset, LANES)]
            matrix = jnp.where(chosen & (of_field == c), 1.0, 0.0).astype(BF16)
            total += jnp.dot(
                part.reshape(chunk * rows, LANES), matrix, preferred_element_type=F32
            )
        total = total.reshape(chunk, rows, LANES)

        @pl.when(step == 0)
        def _():
            out[...] = total

        @pl.when(step > 0)
        def _():
            out[...] += total

    depth = chunk * pl.num_programs(0)

    @pl.when((odd_z == 0) & (step == pl.num_programs(0) - 1))
    def _():
        for n, (c, own, _) in enumerate(layers_to_next(chunk)):
            z_out[n] = own_field(refs, c, own).astype(F32)

    @pl.when((odd_z == 1) & (step == 0))
    def _():
        for n, (c, own, _) in enumerate(layers_to_previous(chunk)):
            z_out[n] = own_field(refs, c, own).astype(F32)


def edge_rows(array, to_next):
    rows = array.shape[0]
    row = row_of((TILE, LANES))
    last = pltpu.roll(array[rows - TILE:], SHIFT, 0)
    first = pltpu.roll(array[:TILE], SHIFT, 0)
    last = jnp.where((row >= SHIFT - WIDE) & (row < SHIFT), last, 0.0)
    first = jnp.where((row >= SHIFT) & (row < SHIFT + WIDE), first, 0.0)
    return jnp.where(to_next == 1, last, first)


def corner_kernel(x_messages, *refs):
    xp, xz = refs[:x_messages], refs[x_messages:2 * x_messages]
    zr, picker, a_out, b_out = refs[2 * x_messages:]
    _, rows, cols = zr.shape
    odd_y = place_on("gy")[1]
    arrived = zr[...].reshape(LAYERS * rows, cols).astype(BF16)
    picked = jnp.dot(picker[odd_y], arrived, preferred_element_type=F32)
    count = LAYERS * WIDE
    for message, out in ((0, a_out), (1, b_out)):
        at = 0
        for t in range(cols // LANES):
            for n in range(0, count, TILE):
                begin = message * count + n
                out[at] = picked[begin:begin + TILE, t * LANES:(t + 1) * LANES]
                at += 1
        for array in (*xp, *xz):
            for k in range(array.shape[0]):
                out[at + k] = edge_rows(array[k], 1 - (odd_y ^ message))
            at += array.shape[0]


def spread(tiles, halo):
    low = row_of((TILE, LANES)) < SHIFT
    turned = [pltpu.roll(t, SHIFT, 0) for t in tiles]
    out = [jnp.where(low, halo, turned[0])]
    for before, after in zip(turned, turned[1:]):
        out.append(jnp.where(low, before, after))
    out.append(jnp.where(low, turned[-1], halo))
    return out


def gather(tiles):
    low = row_of((TILE, LANES)) < SHIFT
    turned = [pltpu.roll(t, SHIFT, 0) for t in tiles]
    return [jnp.where(low, before, after) for before, after in zip(turned, turned[1:])]


def window_kernel(x_messages, inverse, fe, fh, ae, ah, material, height, *others):
    xp, xz = others[:x_messages], others[x_messages:2 * x_messages]
    (zr, ya, yb, corner_a, corner_b, placer, corner_placing, table, grad_out, dual_out, forward_e,
     forward_g, dual_e, dual_g, second_e, third_e, factor) = others[2 * x_messages:]
    depth, rows, cols = material.shape
    own = cols // LANES
    tiles = own + 1
    blocks = rows // TILE + 1
    refs = (fe, fh, ae, ah, material)
    (at_x, odd_x), (at_y, odd_y), (at_z, odd_z) = (place_on(axis) for axis in ("gx", "gy", "gz"))
    start_z = at_z * depth
    row = row_of((TILE, LANES))
    lane = lane_of((TILE, LANES))
    zero = jnp.zeros((TILE, LANES), F32)
    squared = [inverse[m] * (COURANT * COURANT) for m in range(inverse.shape[0])]

    def rows_at(b):
        return pl.ds(b * TILE, TILE)

    def lane_tile(array, t):
        return array[:, t * LANES:(t + 1) * LANES]

    def row_tiles(array):
        return [array[b * TILE:(b + 1) * TILE] for b in range(blocks - 1)]

    def target(c):
        if c == KAPPA:
            return factor, 0
        return (forward_e, forward_g, dual_e, dual_g)[c // 3], c % 3

    def weight(number):
        value = jnp.zeros(number.shape, F32)
        for m, w in enumerate(squared):
            value = jnp.where(number == m + 1, w, value)
        return value

    for t in range(tiles):
        for b in range(blocks):
            for c in range(3):
                forward_g[c, BEFORE - 1, t, rows_at(b)] = zero
                dual_g[c, BEFORE - 1, t, rows_at(b)] = zero
                for ref in (forward_e, dual_e, second_e, third_e):
                    ref[c, depth + BEFORE, t, rows_at(b)] = zero

    corner_tiles = LAYERS * WIDE // TILE
    at = own * corner_tiles
    groups = depth // TILE
    begin_halo = jnp.where(odd_z == 1, BEFORE - WIDE, BEFORE + depth)
    halo_group = jnp.where(odd_z == 1, groups - 1, 0)
    wides = []
    for array in (*xp, *xz):
        blocks_in = []
        for k in range(array.shape[0]):
            blocks_in += spread(row_tiles(array[k]), corner_a[at + k] + corner_b[at + k])
        at += array.shape[0]
        wides.append(jnp.concatenate(blocks_in, axis=0).astype(BF16))

    def columns_of(c, group, arrays):
        total = None
        for number, array in enumerate(arrays):
            way = 1 - (odd_x ^ number)
            of_field, of_target, of_group = (table[way, k:k + 1, :] for k in (0, 2, 3))
            chosen = (of_field == c) & (of_group == group) & (of_target == row_of((LANES, LANES)))
            matrix = jnp.where(chosen, SCALE[c], 0.0).astype(BF16)
            part = lax.dot_general(
                array, matrix, (((1,), (1,)), ((), ())), preferred_element_type=F32
            )
            total = part if total is None else total + part
        total = total.reshape(-1, blocks * TILE, LANES)
        return weight(total) if c == KAPPA else total

    for c in range(COUNT):
        ref, to = target(c)
        for group in range(groups):
            found = columns_of(c, group, wides[:x_messages])
            ref[to, pl.ds(BEFORE + group * TILE, TILE), own] = found
        ref[to, pl.ds(begin_halo, WIDE), own] = columns_of(c, halo_group, wides[x_messages:])

    def store(items):
        for c, slot, t, parts in items:
            ref, at = target(c)
            for b, part in enumerate(parts):
                ref[at, slot, t, rows_at(b)] = part

    def arrange(c, own_tiles, halo):
        if c == KAPPA:
            own_tiles = [weight(p) for p in own_tiles]
            halo = weight(halo)
        elif SCALE[c] != 1.0:
            own_tiles = [p * SCALE[c] for p in own_tiles]
        return spread(own_tiles, halo)

    arrived = jnp.concatenate([
        jnp.concatenate([ref[t * corner_tiles + k] for t in range(own)], axis=1)
        for ref in (corner_a, corner_b) for k in range(corner_tiles)
    ], axis=0).astype(BF16)
    plane_halos = jnp.dot(corner_placing[odd_y], arrived, preferred_element_type=F32)

    def halo_planes(layers):
        for n, (c, _, position) in enumerate(layers):
            items = []
            for t in range(own):
                halo = lane_tile(plane_halos[n * TILE:(n + 1) * TILE], t) * SCALE[c]
                parts = arrange(c, row_tiles(lane_tile(zr[n], t)), halo)
                items.append((c, position + BEFORE, t, parts))
            store(items)

    @pl.when(odd_z == 0)
    def _():
        halo_planes(layers_to_previous(depth))

    @pl.when(odd_z == 1)
    def _():
        halo_planes(layers_to_next(depth))

    def own_planes(step, _):
        items = []
        for k in range(2):
            z = step * 2 + k
            arrived = jnp.concatenate([ya[z], yb[z]], axis=0).astype(BF16)
            halos = jnp.dot(placer[odd_y], arrived, preferred_element_type=F32)
            for c in range(COUNT):
                whole = own_field(refs, c, z).astype(F32)
                for t in range(own):
                    halo = lane_tile(halos[c * TILE:(c + 1) * TILE], t)
                    parts = arrange(c, row_tiles(lane_tile(whole, t)), halo)
                    items.append((c, z + BEFORE, t, parts))
        store(items)
        return 0

    lax.fori_loop(0, depth // 2, own_planes, 0)

    keep_row = jnp.where((row < SHIFT) & (at_y == 0), 0.0, 1.0)
    keep_lane = jnp.where((lane >= LANES // 2) & (at_x == 0), 0.0, 1.0)

    def mask(value, t, b):
        if b == 0:
            value = value * keep_row
        if t == own:
            value = value * keep_lane
        return value

    def ahead_lanes(parts):
        turned = [pltpu.roll(p, LANES - 1, 1) for p in parts]
        return [jnp.where(lane == LANES - 1, turned[(t + 1) % tiles], turned[t]) for t in range(tiles)]

    def behind_lanes(parts):
        turned = [pltpu.roll(p, 1, 1) for p in parts]
        return [jnp.where(lane == 0, turned[(t - 1) % tiles], turned[t]) for t in range(tiles)]

    def reader(ref, slot):
        seen = {}

        def read(c, ahead, t, b):
            if (c, ahead, t, b) not in seen:
                seen[c, ahead, t, b] = ref[c, slot + ahead, t, rows_at(b)]
            return seen[c, ahead, t, b]

        def ahead_rows(c, ahead, t, b):
            if b == blocks - 1:
                return pltpu.roll(read(c, ahead, t, b), TILE - 1, 0)
            return ref[c, slot + ahead, t, pl.ds(b * TILE + 1, TILE)]

        def behind_rows(c, ahead, t, b):
            if b == 0:
                return pltpu.roll(read(c, ahead, t, b), 1, 0)
            return ref[c, slot + ahead, t, pl.ds(b * TILE - 1, TILE)]

        return read, ahead_rows, behind_rows

    def begin(count):
        return BEFORE + jnp.where(odd_z == 1, depth - count, 0)

    def magnetic(e, g, count, emit=None):
        width = own if emit is not None else tiles
        first = begin(count)

        def step(number, _):
            slot = first + number * UNROLL
            read, ahead_rows, _ = reader(e, slot)
            old, _, _ = reader(g, slot)
            results = {}
            for k in range(UNROLL):
                for b in range(blocks):
                    y_x = ahead_lanes([read(1, k, t, b) for t in range(tiles)])
                    z_x = ahead_lanes([read(2, k, t, b) for t in range(tiles)])
                    for t in range(width):
                        ex, ey, ez = (read(c, k, t, b) for c in range(3))
                        curl = (
                            (ahead_rows(2, k, t, b) - ez) - (read(1, k + 1, t, b) - ey),
                            (read(0, k + 1, t, b) - ex) - (z_x[t] - ez),
                            (y_x[t] - ey) - (ahead_rows(0, k, t, b) - ex),
                        )
                        for c in range(3):
                            value = old(c, k, t, b) + curl[c]
                            results[c, k, t, b] = value if emit is not None else mask(value, t, b)
            if emit is not None:
                emit(slot, results)
            else:
                for (c, k, t, b), value in results.items():
                    g[c, slot + k, t, rows_at(b)] = value
            return 0

        lax.fori_loop(0, count // UNROLL, step, 0)

    def electric(e, g, to, count, partner=None, totals=()):
        first = begin(count)

        def step(number, carry):
            carry = list(carry)
            slot = first + number * UNROLL
            read, _, behind_rows = reader(g, slot)
            old, _, _ = reader(e, slot)
            weights, _, _ = reader(factor, slot)
            results = {}
            for k in range(UNROLL):
                if partner is not None:
                    position = slot + k - BEFORE
                    inside = (position >= 0) & (position < depth)
                    position = jnp.where(inside, position + start_z, jnp.int32(2**30))
                for b in range(blocks):
                    y_x = behind_lanes([read(1, k, t, b) for t in range(tiles)])
                    z_x = behind_lanes([read(2, k, t, b) for t in range(tiles)])
                    for t in range(tiles):
                        gx, gy, gz = (read(c, k, t, b) for c in range(3))
                        curl = (
                            (gz - behind_rows(2, k, t, b)) - (gy - read(1, k - 1, t, b)),
                            (gx - read(0, k - 1, t, b)) - (gz - z_x[t]),
                            (gy - y_x[t]) - (gx - behind_rows(0, k, t, b)),
                        )
                        scale = weights(0, k, t, b)
                        product = None
                        for c in range(3):
                            value = old(c, k, t, b) - scale * curl[c]
                            results[c, k, t, b] = value
                            if partner is not None and t < own:
                                term = value * partner[c, slot + k, t, rows_at(b)]
                                product = term if product is None else product + term
                        if product is not None:
                            chosen = position < limits[t * blocks + b]
                            carry[t * blocks + b] += jnp.where(chosen, product, 0.0)
            for (c, k, t, b), value in results.items():
                to[c, slot + k, t, rows_at(b)] = value
            return tuple(carry)

        return lax.fori_loop(0, count // UNROLL, step, totals)

    def emit_dual(slot, results):
        for k in range(UNROLL):
            for c in range(3):
                for t in range(own):
                    values = gather([results[c, k, t, b] for b in range(blocks)])
                    for b, value in enumerate(values):
                        where = (c, slot + k - BEFORE, rows_at(b), pl.ds(t * LANES, LANES))
                        dual_out[where] = value * COURANT

    def count(low, high):
        return -(-(depth + max(low, high)) // UNROLL) * UNROLL

    magnetic(dual_e, dual_g, count(2, 2))
    electric(dual_e, dual_g, second_e, count(1, 2))
    magnetic(second_e, dual_g, count(1, 1))
    electric(second_e, dual_g, third_e, count(0, 1))
    magnetic(third_e, dual_g, depth, emit_dual)

    none = jnp.zeros((TILE, LANES), jnp.int32)
    limits = []
    for t in range(own):
        limits += spread(row_tiles(lane_tile(height[...], t)), none)
    totals = (zero,) * (own * blocks)
    magnetic(forward_e, forward_g, count(3, 2))
    totals = electric(forward_e, forward_g, forward_e, count(2, 2), third_e, totals)
    magnetic(forward_e, forward_g, count(2, 1))
    totals = electric(forward_e, forward_g, forward_e, count(1, 1), second_e, totals)
    magnetic(forward_e, forward_g, count(1, 0))
    totals = electric(forward_e, forward_g, forward_e, depth, dual_e, totals)
    for t in range(own):
        values = gather(list(totals[t * blocks:(t + 1) * blocks]))
        for b, value in enumerate(values):
            grad_out[rows_at(b), t * LANES:(t + 1) * LANES] = value


def local(forward_e, forward_h, adjoint_e, adjoint_h, material, inv_permittivity, height):
    depth, rows, cols = material.shape
    tiles = cols // LANES
    nx, nz = lax.axis_size("gx"), lax.axis_size("gz")
    assert nz == 2
    odd_z = lax.rem(lax.axis_index("gz"), 2)
    picker = jnp.asarray(row_picker(rows), BF16)
    placer = jnp.asarray(row_placer(rows), BF16)
    corner_picking = jnp.asarray(corner_picker(rows), BF16)
    corner_placing = jnp.asarray(corner_placer(), BF16)
    table = jnp.asarray(column_table(depth))
    vmem = pl.BlockSpec(memory_space=pltpu.VMEM)
    smem = pl.BlockSpec(memory_space=pltpu.SMEM)
    params = pltpu.CompilerParams(vmem_limit_bytes=60 * 1024 * 1024)
    x_messages = 1 if nx == 2 else 2

    chunk = TILE
    field_block = pl.BlockSpec((3, chunk, rows, cols), lambda i: (0, i, 0, 0))
    y_block = pl.BlockSpec((chunk, LAYERS, cols), lambda i: (i, 0, 0))
    x_shape = jax.ShapeDtypeStruct((chunk, rows, LANES), F32)
    y_shape = jax.ShapeDtypeStruct((depth, LAYERS, cols), F32)
    packed = pl.pallas_call(
        functools.partial(pack_kernel, x_messages),
        grid=(depth // chunk,),
        out_shape=[x_shape] * x_messages
        + [jax.ShapeDtypeStruct((LAYERS, rows, cols), F32), y_shape, y_shape],
        in_specs=[field_block] * 4
        + [pl.BlockSpec((chunk, rows, cols), lambda i: (i, 0, 0)), vmem, vmem],
        out_specs=[vmem] * (x_messages + 1) + [y_block] * 2,
        compiler_params=params,
        name="pack",
    )(forward_e, forward_h, adjoint_e, adjoint_h, material, picker, table)
    z_message, ya, yb = packed[x_messages:]
    xp = [swap(packed[n], "gx", n) for n in range(x_messages)]
    yb = swap(yb, "gy", 1)
    ya = swap(ya, "gy", 0)
    zr = swap(z_message, "gz", 0)
    edge = jnp.where(odd_z == 0, chunk - WIDE, 0)
    xz = [swap(lax.dynamic_slice_in_dim(x, edge, WIDE, axis=0), "gz", 0) for x in xp]

    corner_tiles = LAYERS * WIDE // TILE * tiles + x_messages * (chunk + WIDE)
    corner_shape = jax.ShapeDtypeStruct((corner_tiles, TILE, LANES), F32)
    corner_a, corner_b = pl.pallas_call(
        functools.partial(corner_kernel, x_messages),
        out_shape=[corner_shape, corner_shape],
        in_specs=[vmem] * (2 * x_messages + 2),
        out_specs=[vmem] * 2,
        compiler_params=params,
        name="corners",
    )(*xp, *xz, zr, corner_picking)
    corner_b = swap(corner_b, "gy", 1)
    corner_a = swap(corner_a, "gy", 0)

    block = (BEFORE + depth + AFTER, tiles + 1, (rows // TILE + 1) * TILE, LANES)
    grad, dual = pl.pallas_call(
        functools.partial(window_kernel, x_messages),
        out_shape=[
            jax.ShapeDtypeStruct((rows, cols), F32),
            jax.ShapeDtypeStruct((3, depth, rows, cols), F32),
        ],
        in_specs=[smem] + [vmem] * (14 + 2 * x_messages),
        out_specs=[vmem] * 2,
        scratch_shapes=[
            *[pltpu.VMEM((3,) + block, F32)] * 6,
            pltpu.VMEM((1,) + block, F32),
        ],
        compiler_params=params,
        name="window",
    )(
        inv_permittivity, forward_e, forward_h, adjoint_e, adjoint_h, material, height,
        *xp, *xz, zr, ya, yb, corner_a, corner_b, placer, corner_placing, table,
    )
    return grad + swap(grad, "gz", 0), dual


def solution(mesh):
    fields = P(None, "gz", "gy", "gx")
    return jax.shard_map(
        local,
        mesh=mesh,
        in_specs=(fields, fields, fields, fields, P("gz", "gy", "gx"), P(), P("gy", "gx")),
        out_specs=(P("gy", "gx"), fields),
        check_vma=False,
    )
```

```python
import functools

import jax
import jax.numpy as jnp
import numpy as np
from jax import lax
from jax.experimental import pallas as pl
from jax.experimental.pallas import tpu as pltpu
from jax.sharding import PartitionSpec as P

STEPS = 3
COURANT = 0.5
LANES = 128
TILE = 8
WIDE = 3
BEFORE = 5
AFTER = 5
UNROLL = 4
SHIFT = 4
COUNT = 13
FE, FH, AE, AH, KAPPA = 0, 3, 6, 9, 12
LOW_DEPTH = [3] * 3 + [3] * 3 + [2] * 3 + [2] * 3 + [2]
HIGH_DEPTH = [3] * 3 + [2] * 3 + [3] * 3 + [2] * 3 + [2]
LAYERS = sum(LOW_DEPTH)
SCALE = [1.0] * 3 + [-1.0 / COURANT] * 3 + [1.0] * 3 + [1.0 / COURANT] * 3 + [1.0]
F32 = jnp.float32
BF16 = jnp.bfloat16


def layers_to_next(length):
    return [(c, length - d + k, k - d) for c, d in enumerate(LOW_DEPTH) for k in range(d)]


def layers_to_previous(length):
    return [(c, k, length + k) for c, d in enumerate(HIGH_DEPTH) for k in range(d)]


def swap_pairs(length, offset):
    pairs = []
    for i in range(offset, length - 1, 2):
        pairs += [(i, i + 1), (i + 1, i)]
    return pairs


def swap(array, axis, offset):
    return lax.ppermute(array, axis, swap_pairs(lax.axis_size(axis), offset))


def two_ways(rows_in, to_next, to_previous):
    first, second = np.zeros((2, len(to_next), rows_in), np.float32)
    for n, index in enumerate(to_next):
        first[n, index] = 1
    for n, index in enumerate(to_previous):
        second[n, index] = 1
    return np.stack([np.concatenate([first, second]), np.concatenate([second, first])])


def row_picker(rows):
    return two_ways(
        COUNT * rows,
        [c * rows + own for c, own, _ in layers_to_next(rows)],
        [c * rows + own for c, own, _ in layers_to_previous(rows)],
    )


def corner_picker(rows):
    return two_ways(
        LAYERS * rows,
        [n * rows + rows - WIDE + k for n in range(LAYERS) for k in range(WIDE)],
        [n * rows + k for n in range(LAYERS) for k in range(WIDE)],
    )


def ways_back(rows_out, low, high):
    first = np.zeros((rows_out, len(low)), np.float32)
    second = np.zeros((rows_out, len(high)), np.float32)
    for n, (index, value) in enumerate(low):
        first[index, n] = value
    for n, (index, value) in enumerate(high):
        second[index, n] = value
    return np.stack([np.concatenate([second, first], 1), np.concatenate([first, second], 1)])


def row_placer(rows):
    low = [(c * TILE + there + SHIFT, SCALE[c]) for c, _, there in layers_to_next(rows)]
    high = [(c * TILE + there - rows + SHIFT, SCALE[c]) for c, _, there in layers_to_previous(rows)]
    return ways_back(COUNT * TILE, low, high)


def corner_placer():
    low = [(n * TILE + SHIFT - WIDE + k, 1) for n in range(LAYERS) for k in range(WIDE)]
    high = [(n * TILE + SHIFT + k, 1) for n in range(LAYERS) for k in range(WIDE)]
    return ways_back(LAYERS * TILE, low, high)


def column_table(depth):
    groups = depth // TILE
    assert groups * LAYERS <= LANES
    table = np.full((2, TILE, LANES), -1, np.int32)
    for way, layers in enumerate((layers_to_next(LANES), layers_to_previous(0))):
        for g in range(groups):
            for n, (c, own, there) in enumerate(layers):
                lane = g * LAYERS + n
                table[way, :4, lane] = c, own, there % LANES, g
    return table


def lane_of(shape):
    return lax.broadcasted_iota(jnp.int32, shape, len(shape) - 1)


def row_of(shape):
    return lax.broadcasted_iota(jnp.int32, shape, len(shape) - 2)


def own_field(refs, c, z):
    fe, fh, ae, ah, material = refs
    if c == KAPPA:
        return (material[z] + 1).astype(F32).astype(BF16)
    return (fe, fh, ae, ah)[c // 3][c % 3, z]


def place_on(axis):
    return lax.axis_index(axis), lax.rem(lax.axis_index(axis), 2)


def pack_kernel(x_messages, fe, fh, ae, ah, material, picker, table, *outs):
    chunk, rows, cols = material.shape
    refs = (fe, fh, ae, ah, material)
    x_out, xz_out = outs[:x_messages], outs[x_messages:2 * x_messages]
    z_out, ya_out, yb_out = outs[2 * x_messages:]
    odd_x, odd_y, odd_z = (place_on(axis)[1] for axis in ("gx", "gy", "gz"))
    step = pl.program_id(0)

    picked = [
        jnp.dot(
            picker[odd_y],
            jnp.concatenate([own_field(refs, c, z) for c in range(COUNT)], axis=0),
            preferred_element_type=F32,
        )
        for z in range(chunk)
    ]
    for z in range(chunk):
        ya_out[z] = picked[z][:LAYERS]
        yb_out[z] = picked[z][LAYERS:]

    for number, out in enumerate(x_out):
        way = odd_x ^ number
        offset = pl.multiple_of((1 - way) * (cols - LANES), LANES)
        total = jnp.zeros((chunk * rows, LANES), F32)
        of_field, of_lane, of_group = (table[way, k:k + 1, :] for k in (0, 1, 3))
        chosen = (row_of((LANES, LANES)) == of_lane) & (of_group == step)
        for c in range(COUNT):
            if c == KAPPA:
                part = material[:, :, pl.ds(offset, LANES)]
                part = (part + 1).astype(F32).astype(BF16)
            else:
                part = (fe, fh, ae, ah)[c // 3][c % 3, :, :, pl.ds(offset, LANES)]
            matrix = jnp.where(chosen & (of_field == c), 1.0, 0.0).astype(BF16)
            total += jnp.dot(
                part.reshape(chunk * rows, LANES), matrix, preferred_element_type=F32
            )
        total = total.reshape(chunk, rows, LANES)

        @pl.when(step == 0)
        def _():
            out[...] = total

        @pl.when(step > 0)
        def _():
            out[...] += total

    def edges(layers):
        for n, (c, own, _) in enumerate(layers):
            z_out[n] = own_field(refs, c, own).astype(F32)

    @pl.when((odd_z == 0) & (step == pl.num_programs(0) - 1))
    def _():
        edges(layers_to_next(chunk))

    @pl.when((odd_z == 1) & (step == 0))
    def _():
        edges(layers_to_previous(chunk))

    @pl.when(step == pl.num_programs(0) - 1)
    def _():
        edge = jnp.where(odd_z == 0, chunk - WIDE, 0)
        for whole, part in zip(x_out, xz_out):
            part[...] = whole[pl.ds(edge, WIDE)]


def edge_rows(array, to_next):
    rows = array.shape[0]
    row = row_of((TILE, LANES))
    last = pltpu.roll(array[rows - TILE:], SHIFT, 0)
    first = pltpu.roll(array[:TILE], SHIFT, 0)
    last = jnp.where((row >= SHIFT - WIDE) & (row < SHIFT), last, 0.0)
    first = jnp.where((row >= SHIFT) & (row < SHIFT + WIDE), first, 0.0)
    return jnp.where(to_next == 1, last, first)


def corner_kernel(x_messages, *refs):
    arrays = refs[:2 * x_messages]
    zr, picker, a_out, b_out = refs[2 * x_messages:]
    _, rows, cols = zr.shape
    odd_y = place_on("gy")[1]
    arrived = zr[...].reshape(LAYERS * rows, cols).astype(BF16)
    picked = jnp.dot(picker[odd_y], arrived, preferred_element_type=F32)
    count = LAYERS * WIDE
    for message, out in ((0, a_out), (1, b_out)):
        at = 0
        for t in range(cols // LANES):
            for n in range(message * count, (message + 1) * count, TILE):
                out[at] = lane_tile(picked[n:n + TILE], t)
                at += 1
        for array in arrays:
            for k in range(array.shape[0]):
                out[at + k] = edge_rows(array[k], 1 - (odd_y ^ message))
            at += array.shape[0]


def spread(tiles, halo):
    low = row_of((TILE, LANES)) < SHIFT
    turned = [pltpu.roll(t, SHIFT, 0) for t in tiles]
    out = [jnp.where(low, halo, turned[0])]
    for before, after in zip(turned, turned[1:]):
        out.append(jnp.where(low, before, after))
    out.append(jnp.where(low, turned[-1], halo))
    return out


def gather(tiles):
    low = row_of((TILE, LANES)) < SHIFT
    turned = [pltpu.roll(t, SHIFT, 0) for t in tiles]
    return [jnp.where(low, before, after) for before, after in zip(turned, turned[1:])]


def lane_tile(array, t):
    return array[:, t * LANES:(t + 1) * LANES]


def row_tiles(array):
    return [array[b:b + TILE] for b in range(0, array.shape[0], TILE)]


def rows_at(b):
    return pl.ds(b * TILE, TILE)


def weight(number, inverse):
    value = jnp.zeros(number.shape, F32)
    for m in range(inverse.shape[0]):
        value = jnp.where(number == m + 1, inverse[m] * (COURANT * COURANT), value)
    return value


def arrange(c, own_tiles, halo, inverse):
    if c == KAPPA:
        own_tiles = [weight(p, inverse) for p in own_tiles]
        halo = weight(halo, inverse)
    elif SCALE[c] != 1.0:
        own_tiles = [p * SCALE[c] for p in own_tiles]
        halo = halo * SCALE[c]
    return spread(own_tiles, halo)


def prepare_kernel(inverse, fe, fh, ae, ah, material, *state):
    chunk, rows, cols = material.shape
    refs = (fe, fh, ae, ah, material)
    first = BEFORE + pl.program_id(0) * chunk
    zero = jnp.zeros((TILE, LANES), F32)
    for z in range(chunk):
        items = []
        for c in range(COUNT):
            whole = own_field(refs, c, z).astype(F32)
            for t in range(cols // LANES):
                items.append((c, t, arrange(c, row_tiles(lane_tile(whole, t)), zero, inverse)))
        for c, t, parts in items:
            for b, part in enumerate(parts):
                state[c // 3][c % 3, first + z, t, rows_at(b)] = part


def window_kernel(x_messages, inverse, height, *others):
    xp, xz = others[:x_messages], others[x_messages:2 * x_messages]
    (zr, ya, yb, corner_a, corner_b, placer, corner_placing, table) = others[
        2 * x_messages:2 * x_messages + 8]
    (grad_out, dual_out, forward_e, forward_g, dual_e, dual_g, factor, second_e, third_e) = others[
        2 * x_messages + 13:]
    rows, cols = height.shape
    depth = ya.shape[0]
    own = cols // LANES
    tiles = own + 1
    blocks = rows // TILE + 1
    (at_x, odd_x), (at_y, odd_y), (at_z, odd_z) = (place_on(axis) for axis in ("gx", "gy", "gz"))
    start_z = at_z * depth
    row = row_of((TILE, LANES))
    lane = lane_of((TILE, LANES))
    zero = jnp.zeros((TILE, LANES), F32)
    state = (forward_e, forward_g, dual_e, dual_g, factor)

    for t in range(tiles):
        for b in range(blocks):
            for c in range(3):
                forward_g[c, BEFORE - 1, t, rows_at(b)] = zero
                dual_g[c, BEFORE - 1, t, rows_at(b)] = zero
                for ref in (forward_e, dual_e, second_e, third_e):
                    ref[c, depth + BEFORE, t, rows_at(b)] = zero

    corner_tiles = LAYERS * WIDE // TILE
    at = own * corner_tiles
    groups = depth // TILE
    begin_halo = jnp.where(odd_z == 1, BEFORE - WIDE, BEFORE + depth)
    halo_group = jnp.where(odd_z == 1, groups - 1, 0)
    wides = []
    for array in (*xp, *xz):
        blocks_in = []
        for k in range(array.shape[0]):
            blocks_in += spread(row_tiles(array[k]), corner_a[at + k] + corner_b[at + k])
        at += array.shape[0]
        wides.append(jnp.concatenate(blocks_in, axis=0).astype(BF16))

    def columns_of(c, group, arrays):
        total = None
        for number, array in enumerate(arrays):
            way = 1 - (odd_x ^ number)
            of_field, of_target, of_group = (table[way, k:k + 1, :] for k in (0, 2, 3))
            chosen = (of_field == c) & (of_group == group) & (of_target == row_of((LANES, LANES)))
            matrix = jnp.where(chosen, SCALE[c], 0.0).astype(BF16)
            part = lax.dot_general(
                array, matrix, (((1,), (1,)), ((), ())), preferred_element_type=F32
            )
            total = part if total is None else total + part
        total = total.reshape(-1, blocks * TILE, LANES)
        return weight(total, inverse) if c == KAPPA else total

    for c in range(COUNT):
        ref, to = state[c // 3], c % 3
        for group in range(groups):
            found = columns_of(c, group, wides[:x_messages])
            ref[to, pl.ds(BEFORE + group * TILE, TILE), own] = found
        ref[to, pl.ds(begin_halo, WIDE), own] = columns_of(c, halo_group, wides[x_messages:])

    arrived = jnp.concatenate([
        jnp.concatenate([ref[t * corner_tiles + k] for t in range(own)], axis=1)
        for ref in (corner_a, corner_b) for k in range(corner_tiles)
    ], axis=0).astype(BF16)
    plane_halos = jnp.dot(corner_placing[odd_y], arrived, preferred_element_type=F32)

    def halo_planes(layers):
        for n, (c, _, position) in enumerate(layers):
            for t in range(own):
                halo = lane_tile(plane_halos[n * TILE:(n + 1) * TILE], t)
                parts = arrange(c, row_tiles(lane_tile(zr[n], t)), halo, inverse)
                for b, part in enumerate(parts):
                    state[c // 3][c % 3, position + BEFORE, t, rows_at(b)] = part

    @pl.when(odd_z == 0)
    def _():
        halo_planes(layers_to_previous(depth))

    @pl.when(odd_z == 1)
    def _():
        halo_planes(layers_to_next(depth))

    def row_halos(step, _):
        for k in range(4):
            z = step * 4 + k
            arrived = jnp.concatenate([ya[z], yb[z]], axis=0).astype(BF16)
            halos = jnp.dot(placer[odd_y], arrived, preferred_element_type=F32)
            for c in range(COUNT):
                for t in range(own):
                    halo = lane_tile(halos[c * TILE:(c + 1) * TILE], t)
                    if c == KAPPA:
                        halo = weight(halo, inverse)
                    ref, at = state[c // 3], (c % 3, z + BEFORE, t)
                    ref[(*at, pl.ds(0, SHIFT))] = halo[:SHIFT]
                    ref[(*at, pl.ds(blocks * TILE - SHIFT, SHIFT))] = halo[SHIFT:]
        return 0

    lax.fori_loop(0, depth // 4, row_halos, 0)

    keep_row = jnp.where((row < SHIFT) & (at_y == 0), 0.0, 1.0)
    keep_lane = jnp.where((lane >= LANES // 2) & (at_x == 0), 0.0, 1.0)

    def mask(value, t, b):
        if b == 0:
            value = value * keep_row
        if t == own:
            value = value * keep_lane
        return value

    def ahead_lanes(parts):
        turned = [pltpu.roll(p, LANES - 1, 1) for p in parts]
        return [jnp.where(lane == LANES - 1, turned[(t + 1) % tiles], turned[t]) for t in range(tiles)]

    def behind_lanes(parts):
        turned = [pltpu.roll(p, 1, 1) for p in parts]
        return [jnp.where(lane == 0, turned[(t - 1) % tiles], turned[t]) for t in range(tiles)]

    def reader(ref, slot):
        seen = {}

        def read(c, ahead, t, b):
            if (c, ahead, t, b) not in seen:
                seen[c, ahead, t, b] = ref[c, slot + ahead, t, rows_at(b)]
            return seen[c, ahead, t, b]

        def ahead_rows(c, ahead, t, b):
            if b == blocks - 1:
                return pltpu.roll(read(c, ahead, t, b), TILE - 1, 0)
            return ref[c, slot + ahead, t, pl.ds(b * TILE + 1, TILE)]

        def behind_rows(c, ahead, t, b):
            if b == 0:
                return pltpu.roll(read(c, ahead, t, b), 1, 0)
            return ref[c, slot + ahead, t, pl.ds(b * TILE - 1, TILE)]

        return read, ahead_rows, behind_rows

    def begin(count):
        return BEFORE + jnp.where(odd_z == 1, depth - count, 0)

    def magnetic(e, g, count, emit=None):
        width = own if emit is not None else tiles
        first = begin(count)

        def step(number, _):
            slot = first + number * UNROLL
            read, ahead_rows, _ = reader(e, slot)
            old, _, _ = reader(g, slot)
            results = {}
            for k in range(UNROLL):
                for b in range(blocks):
                    y_x = ahead_lanes([read(1, k, t, b) for t in range(tiles)])
                    z_x = ahead_lanes([read(2, k, t, b) for t in range(tiles)])
                    for t in range(width):
                        ex, ey, ez = (read(c, k, t, b) for c in range(3))
                        curl = (
                            (ahead_rows(2, k, t, b) - ez) - (read(1, k + 1, t, b) - ey),
                            (read(0, k + 1, t, b) - ex) - (z_x[t] - ez),
                            (y_x[t] - ey) - (ahead_rows(0, k, t, b) - ex),
                        )
                        for c in range(3):
                            value = old(c, k, t, b) + curl[c]
                            results[c, k, t, b] = value if emit is not None else mask(value, t, b)
            if emit is not None:
                emit(slot, results)
            else:
                for (c, k, t, b), value in results.items():
                    g[c, slot + k, t, rows_at(b)] = value
            return 0

        lax.fori_loop(0, count // UNROLL, step, 0)

    def electric(e, g, to, count, partner=None, totals=()):
        first = begin(count)

        def step(number, carry):
            carry = list(carry)
            slot = first + number * UNROLL
            read, _, behind_rows = reader(g, slot)
            old, _, _ = reader(e, slot)
            weights, _, _ = reader(factor, slot)
            results = {}
            for k in range(UNROLL):
                if partner is not None:
                    position = slot + k - BEFORE
                    inside = (position >= 0) & (position < depth)
                    position = jnp.where(inside, position + start_z, jnp.int32(2**30))
                for b in range(blocks):
                    y_x = behind_lanes([read(1, k, t, b) for t in range(tiles)])
                    z_x = behind_lanes([read(2, k, t, b) for t in range(tiles)])
                    for t in range(tiles):
                        gx, gy, gz = (read(c, k, t, b) for c in range(3))
                        curl = (
                            (gz - behind_rows(2, k, t, b)) - (gy - read(1, k - 1, t, b)),
                            (gx - read(0, k - 1, t, b)) - (gz - z_x[t]),
                            (gy - y_x[t]) - (gx - behind_rows(0, k, t, b)),
                        )
                        scale = weights(0, k, t, b)
                        product = None
                        for c in range(3):
                            value = old(c, k, t, b) - scale * curl[c]
                            results[c, k, t, b] = value
                            if partner is not None and t < own:
                                term = value * partner[c, slot + k, t, rows_at(b)]
                                product = term if product is None else product + term
                        if product is not None:
                            chosen = position < limits[t * blocks + b]
                            carry[t * blocks + b] += jnp.where(chosen, product, 0.0)
            for (c, k, t, b), value in results.items():
                to[c, slot + k, t, rows_at(b)] = value
            return tuple(carry)

        return lax.fori_loop(0, count // UNROLL, step, totals)

    def emit_dual(slot, results):
        for k in range(UNROLL):
            for c in range(3):
                for t in range(own):
                    values = gather([results[c, k, t, b] for b in range(blocks)])
                    for b, value in enumerate(values):
                        where = (c, slot + k - BEFORE, rows_at(b), pl.ds(t * LANES, LANES))
                        dual_out[where] = value * COURANT

    def count(low, high):
        return -(-(depth + max(low, high)) // UNROLL) * UNROLL

    magnetic(dual_e, dual_g, count(2, 2))
    electric(dual_e, dual_g, second_e, count(1, 2))
    magnetic(second_e, dual_g, count(1, 1))
    electric(second_e, dual_g, third_e, count(0, 1))
    magnetic(third_e, dual_g, depth, emit_dual)

    none = jnp.zeros((TILE, LANES), jnp.int32)
    limits = []
    for t in range(own):
        limits += spread(row_tiles(lane_tile(height[...], t)), none)
    totals = (zero,) * (own * blocks)
    magnetic(forward_e, forward_g, count(3, 2))
    totals = electric(forward_e, forward_g, forward_e, count(2, 2), third_e, totals)
    magnetic(forward_e, forward_g, count(2, 1))
    totals = electric(forward_e, forward_g, forward_e, count(1, 1), second_e, totals)
    magnetic(forward_e, forward_g, count(1, 0))
    totals = electric(forward_e, forward_g, forward_e, depth, dual_e, totals)
    for t in range(own):
        values = gather(list(totals[t * blocks:(t + 1) * blocks]))
        for b, value in enumerate(values):
            grad_out[rows_at(b), t * LANES:(t + 1) * LANES] = value


def corner_swap(array, axes, offsets):
    lengths = [lax.axis_size(a) for a in axes]
    pairs = [
        (i * lengths[1] + j, k * lengths[1] + l)
        for i, k in swap_pairs(lengths[0], offsets[0])
        for j, l in swap_pairs(lengths[1], offsets[1])
    ]
    return lax.ppermute(array, axes, pairs)


def local(forward_e, forward_h, adjoint_e, adjoint_h, material, inv_permittivity, height):
    depth, rows, cols = material.shape
    tiles = cols // LANES
    nx, nz = lax.axis_size("gx"), lax.axis_size("gz")
    assert nz == 2
    picker = jnp.asarray(row_picker(rows), BF16)
    placer = jnp.asarray(row_placer(rows), BF16)
    corner_picking = jnp.asarray(corner_picker(rows), BF16)
    corner_placing = jnp.asarray(corner_placer(), BF16)
    table = jnp.asarray(column_table(depth))
    vmem = pl.BlockSpec(memory_space=pltpu.VMEM)
    smem = pl.BlockSpec(memory_space=pltpu.SMEM)
    params = pltpu.CompilerParams(vmem_limit_bytes=24 * 1024 * 1024)
    x_messages = 1 if nx == 2 else 2

    chunk = TILE
    field_block = pl.BlockSpec((3, chunk, rows, cols), lambda i: (0, i, 0, 0))
    material_block = pl.BlockSpec((chunk, rows, cols), lambda i: (i, 0, 0))
    y_block = pl.BlockSpec((chunk, LAYERS, cols), lambda i: (i, 0, 0))
    x_shape = jax.ShapeDtypeStruct((chunk, rows, LANES), F32)
    xz_shape = jax.ShapeDtypeStruct((WIDE, rows, LANES), F32)
    y_shape = jax.ShapeDtypeStruct((depth, LAYERS, cols), F32)
    fields = (forward_e, forward_h, adjoint_e, adjoint_h, material)
    packed = pl.pallas_call(
        functools.partial(pack_kernel, x_messages),
        grid=(depth // chunk,),
        out_shape=[x_shape] * x_messages + [xz_shape] * x_messages
        + [jax.ShapeDtypeStruct((LAYERS, rows, cols), F32), y_shape, y_shape],
        in_specs=[field_block] * 4 + [material_block] + [vmem] * 2,
        out_specs=[vmem] * (2 * x_messages + 1) + [y_block] * 2,
        compiler_params=pltpu.CompilerParams(vmem_limit_bytes=60 * 1024 * 1024),
        name="pack",
    )(*fields, picker, table)
    z_message, ya, yb = packed[2 * x_messages:]
    xp = [swap(packed[n], "gx", n) for n in range(x_messages)]
    xz = [corner_swap(packed[x_messages + n], ("gx", "gz"), (n, 0)) for n in range(x_messages)]
    yb = swap(yb, "gy", 1)
    ya = swap(ya, "gy", 0)
    zr = swap(z_message, "gz", 0)

    block = (BEFORE + depth + AFTER, tiles + 1, (rows // TILE + 1) * TILE, LANES)
    state_shapes = [pltpu.VMEM((3,) + block, F32)] * 4 + [pltpu.VMEM((1,) + block, F32)]
    state = pl.pallas_call(
        prepare_kernel,
        grid=(depth // chunk,),
        out_shape=state_shapes,
        in_specs=[smem] + [field_block] * 4 + [material_block],
        out_specs=[vmem] * 5,
        compiler_params=params,
        name="prepare",
    )(inv_permittivity, *fields)

    corner_tiles = LAYERS * WIDE // TILE * tiles + x_messages * (chunk + WIDE)
    corner_shape = jax.ShapeDtypeStruct((corner_tiles, TILE, LANES), F32)
    corner_a, corner_b = pl.pallas_call(
        functools.partial(corner_kernel, x_messages),
        out_shape=[corner_shape, corner_shape],
        in_specs=[vmem] * (2 * x_messages + 2),
        out_specs=[vmem] * 2,
        compiler_params=params,
        name="corners",
    )(*xp, *xz, zr, corner_picking)
    corner_b = swap(corner_b, "gy", 1)
    corner_a = swap(corner_a, "gy", 0)

    operands = (
        inv_permittivity, height, *xp, *xz, zr, ya, yb, corner_a, corner_b, placer,
        corner_placing, table,
    )
    grad, dual = pl.pallas_call(
        functools.partial(window_kernel, x_messages),
        out_shape=[
            jax.ShapeDtypeStruct((rows, cols), F32),
            jax.ShapeDtypeStruct((3, depth, rows, cols), F32),
            *state_shapes,
        ],
        in_specs=[smem] + [vmem] * (len(operands) + 4),
        out_specs=[vmem] * 7,
        input_output_aliases={len(operands) + n: 2 + n for n in range(5)},
        scratch_shapes=[pltpu.VMEM((3,) + block, F32)] * 2,
        compiler_params=params,
        name="window",
    )(*operands, *state)[:2]
    return grad + swap(grad, "gz", 0), dual


def solution(mesh):
    fields = P(None, "gz", "gy", "gx")
    return jax.shard_map(
        local,
        mesh=mesh,
        in_specs=(fields, fields, fields, fields, P("gz", "gy", "gx"), P(), P("gy", "gx")),
        out_specs=(P("gy", "gx"), fields),
        check_vma=False,
    )
```

```python
import functools

import jax
import jax.numpy as jnp
import numpy as np
from jax import lax
from jax.experimental import pallas as pl
from jax.experimental.pallas import tpu as pltpu
from jax.sharding import PartitionSpec as P

STEPS = 3
COURANT = 0.5
LANES = 128
TILE = 8
WIDE = 3
BEFORE = 5
AFTER = 5
SHIFT = 4
COUNT = 13
FE, FH, AE, AH, KAPPA = 0, 3, 6, 9, 12
LOW_DEPTH = [3] * 3 + [3] * 3 + [2] * 3 + [2] * 3 + [2]
HIGH_DEPTH = [3] * 3 + [2] * 3 + [3] * 3 + [2] * 3 + [2]
LAYERS = sum(LOW_DEPTH)
SCALE = [1.0] * 3 + [-1.0 / COURANT] * 3 + [1.0] * 3 + [1.0 / COURANT] * 3 + [1.0]
F32 = jnp.float32
BF16 = jnp.bfloat16


def layers_to_next(length):
    return [(c, length - d + k, k - d) for c, d in enumerate(LOW_DEPTH) for k in range(d)]


def layers_to_previous(length):
    return [(c, k, length + k) for c, d in enumerate(HIGH_DEPTH) for k in range(d)]


def swap_pairs(length, offset):
    pairs = []
    for i in range(offset, length - 1, 2):
        pairs += [(i, i + 1), (i + 1, i)]
    return pairs


def swap(array, axis, offset):
    return lax.ppermute(array, axis, swap_pairs(lax.axis_size(axis), offset))


def two_ways(rows_in, to_next, to_previous):
    first, second = np.zeros((2, len(to_next), rows_in), np.float32)
    for n, index in enumerate(to_next):
        first[n, index] = 1
    for n, index in enumerate(to_previous):
        second[n, index] = 1
    return np.stack([np.concatenate([first, second]), np.concatenate([second, first])])


def row_picker(rows):
    return two_ways(
        COUNT * rows,
        [c * rows + own for c, own, _ in layers_to_next(rows)],
        [c * rows + own for c, own, _ in layers_to_previous(rows)],
    )


def corner_picker(rows):
    group = LANES // rows
    return two_ways(
        LANES,
        [n * rows + rows - WIDE + k for n in range(group) for k in range(WIDE)],
        [n * rows + k for n in range(group) for k in range(WIDE)],
    )


def ways_back(rows_out, low, high):
    first = np.zeros((rows_out, len(low)), np.float32)
    second = np.zeros((rows_out, len(high)), np.float32)
    for n, (index, value) in enumerate(low):
        first[index, n] = value
    for n, (index, value) in enumerate(high):
        second[index, n] = value
    return np.stack([np.concatenate([second, first], 1), np.concatenate([first, second], 1)])


def row_placer(rows):
    low = [(c * TILE + there + SHIFT, SCALE[c]) for c, _, there in layers_to_next(rows)]
    high = [(c * TILE + there - rows + SHIFT, SCALE[c]) for c, _, there in layers_to_previous(rows)]
    return ways_back(COUNT * TILE, low, high)


def corner_placer(rows):
    group = LANES // rows
    low = [(n * TILE + SHIFT - WIDE + k, 1) for n in range(group) for k in range(WIDE)]
    high = [(n * TILE + SHIFT + k, 1) for n in range(group) for k in range(WIDE)]
    return ways_back(group * TILE, low, high)


def column_table(depth):
    groups = depth // TILE
    assert groups * LAYERS <= LANES
    table = np.full((2, TILE, LANES), -1, np.int32)
    for way, layers in enumerate((layers_to_next(LANES), layers_to_previous(0))):
        for g in range(groups):
            for n, (c, own, there) in enumerate(layers):
                lane = g * LAYERS + n
                table[way, :4, lane] = c, own, there % LANES, g
    return table


def lane_of(shape):
    return lax.broadcasted_iota(jnp.int32, shape, len(shape) - 1)


def row_of(shape):
    return lax.broadcasted_iota(jnp.int32, shape, len(shape) - 2)


def own_field(refs, c, z):
    fe, fh, ae, ah, material = refs
    if c == KAPPA:
        return (material[z] + 1).astype(F32).astype(BF16)
    return (fe, fh, ae, ah)[c // 3][c % 3, z]


def place_on(axis):
    return lax.axis_index(axis), lax.rem(lax.axis_index(axis), 2)


def pack_kernel(x_messages, *refs):
    whole, (picker, table), refs = refs[:5], refs[5:7], refs[7:]
    fields, refs = refs[:5], refs[5:]
    x_out, xz_out = refs[:x_messages], refs[x_messages:2 * x_messages]
    z_out, ya_out, yb_low_out, yb_high_out, arrived = refs[2 * x_messages:]
    depth, rows, cols = fields[4].shape
    odd_x, odd_y, odd_z = (place_on(axis)[1] for axis in ("gx", "gy", "gz"))
    groups = depth // TILE

    copies = []
    for group in range(groups):
        planes = pl.ds(group * TILE, TILE)
        parts = [(n, c, planes) for n in range(4) for c in range(3)] + [(4, planes)]
        copies.append([
            pltpu.make_async_copy(
                whole[n].at[at], fields[n].at[at], arrived.at[group, number]
            )
            for number, (n, *at) in enumerate((p[0], *p[1:]) for p in parts)
            for at in [tuple(at)]
        ])
    for group in copies:
        for copy in group:
            copy.start()

    totals = [jnp.zeros((TILE * rows, LANES), F32)] * x_messages
    for group in range(groups):
        for copy in copies[group]:
            copy.wait()
        for z in range(group * TILE, (group + 1) * TILE):
            stacked = jnp.concatenate([own_field(fields, c, z) for c in range(COUNT)], axis=0)
            picked = jnp.dot(picker[odd_y], stacked, preferred_element_type=F32)
            ya_out[z] = picked[:LAYERS]
            half = yb_low_out.shape[0]
            if z < half:
                yb_low_out[z] = picked[LAYERS:]
            else:
                yb_high_out[z - half] = picked[LAYERS:]

        for number in range(x_messages):
            way = odd_x ^ number
            offset = pl.multiple_of((1 - way) * (cols - LANES), LANES)
            of_field, of_lane, of_group = (table[way, k:k + 1, :] for k in (0, 1, 3))
            chosen = (row_of((LANES, LANES)) == of_lane) & (of_group == group)
            planes = pl.ds(group * TILE, TILE)
            for c in range(COUNT):
                if c == KAPPA:
                    part = fields[4][planes, :, pl.ds(offset, LANES)]
                    part = (part + 1).astype(F32).astype(BF16)
                else:
                    part = fields[c // 3][c % 3, planes, :, pl.ds(offset, LANES)]
                matrix = jnp.where(chosen & (of_field == c), 1.0, 0.0).astype(BF16)
                totals[number] += jnp.dot(
                    part.reshape(TILE * rows, LANES), matrix, preferred_element_type=F32
                )

    edge = jnp.where(odd_z == 0, TILE - WIDE, 0)
    for total, out, part in zip(totals, x_out, xz_out):
        out[...] = total.reshape(TILE, rows, LANES)
        part[...] = out[pl.ds(edge, WIDE)]

    def edges(layers):
        for n, (c, own, _) in enumerate(layers):
            z_out[n] = own_field(fields, c, own).astype(F32)

    @pl.when(odd_z == 0)
    def _():
        edges(layers_to_next(depth))

    @pl.when(odd_z == 1)
    def _():
        edges(layers_to_previous(depth))


def edge_rows(array, to_next):
    rows = array.shape[0]
    row = row_of((TILE, LANES))
    last = pltpu.roll(array[rows - TILE:], SHIFT, 0)
    first = pltpu.roll(array[:TILE], SHIFT, 0)
    last = jnp.where((row >= SHIFT - WIDE) & (row < SHIFT), last, 0.0)
    first = jnp.where((row >= SHIFT) & (row < SHIFT + WIDE), first, 0.0)
    return jnp.where(to_next == 1, last, first)


def corner_kernel(x_messages, *refs):
    arrays = refs[:2 * x_messages]
    zr, picker, _, a_out, b_out = refs[2 * x_messages:]
    _, rows, cols = zr.shape
    odd_y = place_on("gy")[1]
    arrived = zr[...].reshape(LAYERS * rows, cols).astype(BF16)
    picked = [
        jnp.dot(picker[odd_y], arrived[n:n + LANES], preferred_element_type=F32)
        for n in range(0, LAYERS * rows, LANES)
    ]
    count = picker.shape[1] // 2
    for message, out in ((0, a_out), (1, b_out)):
        at = 0
        for t in range(cols // LANES):
            for group in picked:
                for n in range(message * count, (message + 1) * count, TILE):
                    out[at] = lane_tile(group[n:n + TILE], t)
                    at += 1
        for array in arrays:
            for k in range(array.shape[0]):
                out[at + k] = edge_rows(array[k], 1 - (odd_y ^ message))
            at += array.shape[0]


def spread(tiles, halo):
    low = row_of((TILE, LANES)) < SHIFT
    turned = [pltpu.roll(t, SHIFT, 0) for t in tiles]
    out = [jnp.where(low, halo, turned[0])]
    for before, after in zip(turned, turned[1:]):
        out.append(jnp.where(low, before, after))
    out.append(jnp.where(low, turned[-1], halo))
    return out


def gather(tiles):
    low = row_of((TILE, LANES)) < SHIFT
    turned = [pltpu.roll(t, SHIFT, 0) for t in tiles]
    return [jnp.where(low, before, after) for before, after in zip(turned, turned[1:])]


def planes_at_once(count):
    return max(n for n in range(1, 18) if count % n == 0)


def lane_tile(array, t):
    return array[:, t * LANES:(t + 1) * LANES]


def row_tiles(array):
    return [array[b:b + TILE] for b in range(0, array.shape[0], TILE)]


def rows_at(b):
    return pl.ds(b * TILE, TILE)


def weight(number, inverse):
    value = jnp.zeros(number.shape, F32)
    for m in range(inverse.shape[0]):
        value = jnp.where(number == m + 1, inverse[m] * (COURANT * COURANT), value)
    return value


def arrange(c, own_tiles, halo, inverse):
    if c == KAPPA:
        own_tiles = [weight(p, inverse) for p in own_tiles]
        halo = weight(halo, inverse)
    elif SCALE[c] != 1.0:
        own_tiles = [p * SCALE[c] for p in own_tiles]
        halo = halo * SCALE[c]
    return spread(own_tiles, halo)


def prepare_kernel(inverse, fe, fh, ae, ah, material, *state):
    depth, _, cols = material.shape
    refs = (fe, fh, ae, ah, material)
    zero = jnp.zeros((TILE, LANES), F32)

    def planes(step, _):
        for k in range(4):
            z = step * 4 + k
            for c in range(COUNT):
                whole = own_field(refs, c, z).astype(F32)
                for t in range(cols // LANES):
                    parts = arrange(c, row_tiles(lane_tile(whole, t)), zero, inverse)
                    for b, part in enumerate(parts):
                        state[c // 3][c % 3, BEFORE + z, t, rows_at(b)] = part
        return 0

    lax.fori_loop(0, depth // 4, planes, 0)


def column_matrix(table, odd_x, number, c, group):
    way = 1 - (odd_x ^ number)
    of_field, of_target, of_group = (table[way, k:k + 1, :] for k in (0, 2, 3))
    chosen = (of_field == c) & (of_group == group) & (of_target == row_of((LANES, LANES)))
    return jnp.where(chosen, SCALE[c], 0.0).astype(BF16)


def columns_of(table, odd_x, c, group, arrays, inverse):
    total = None
    for number, array in enumerate(arrays):
        part = lax.dot_general(
            array, column_matrix(table, odd_x, number, c, group), (((1,), (1,)), ((), ())),
            preferred_element_type=F32,
        )
        total = part if total is None else total + part
    return weight(total, inverse) if c == KAPPA else total


def plane_kernel(x_messages, inverse, *others):
    xp, xz = others[:x_messages], others[x_messages:2 * x_messages]
    zr, table = others[2 * x_messages:2 * x_messages + 2]
    state = others[2 * x_messages + 7:]
    _, rows, cols = zr.shape
    own = cols // LANES
    blocks = rows // TILE + 1
    depth = state[0].shape[1] - BEFORE - AFTER
    odd_x, odd_z = (place_on(axis)[1] for axis in ("gx", "gz"))
    zero = jnp.zeros((TILE, LANES), F32)

    for t in range(own + 1):
        for b in range(blocks):
            for c in range(3):
                for ref, slot in zip(state, (depth + BEFORE, BEFORE - 1) * 2):
                    ref[c, slot, t, rows_at(b)] = zero

    groups = depth // TILE
    begin_halo = jnp.where(odd_z == 1, BEFORE - WIDE, BEFORE + depth)
    halo_group = jnp.where(odd_z == 1, groups - 1, 0)
    wides = []
    for array in (*xp, *xz):
        parts = []
        for k in range(array.shape[0]):
            parts += spread(row_tiles(array[k]), zero)
        wides.append(jnp.concatenate(parts, axis=0).astype(BF16))
    for c in range(COUNT):
        ref, to = state[c // 3], c % 3
        for group in range(groups):
            found = columns_of(table, odd_x, c, group, wides[:x_messages], inverse)
            found = found.reshape(TILE, blocks * TILE, LANES)
            ref[to, pl.ds(BEFORE + group * TILE, TILE), own] = found
        found = columns_of(table, odd_x, c, halo_group, wides[x_messages:], inverse)
        ref[to, pl.ds(begin_halo, WIDE), own] = found.reshape(WIDE, blocks * TILE, LANES)

    def halo_planes(layers):
        for n, (c, _, position) in enumerate(layers):
            for t in range(own):
                parts = arrange(c, row_tiles(lane_tile(zr[n], t)), zero, inverse)
                for b, part in enumerate(parts):
                    state[c // 3][c % 3, position + BEFORE, t, rows_at(b)] = part

    @pl.when(odd_z == 0)
    def _():
        halo_planes(layers_to_previous(depth))

    @pl.when(odd_z == 1)
    def _():
        halo_planes(layers_to_next(depth))


def first_slot(count, depth, odd_z):
    return BEFORE + jnp.where(odd_z == 1, depth - count, 0)


def ahead_lanes(parts):
    lane = lane_of((TILE, LANES))
    turned = [pltpu.roll(p, LANES - 1, 1) for p in parts]
    after = turned[1:] + turned[:1]
    return [jnp.where(lane == LANES - 1, a, t) for a, t in zip(after, turned)]


def reader(ref, slot):
    blocks = ref.shape[3] // TILE
    seen = {}

    def read(c, ahead, t, b):
        if (c, ahead, t, b) not in seen:
            seen[c, ahead, t, b] = ref[c, slot + ahead, t, rows_at(b)]
        return seen[c, ahead, t, b]

    def ahead_rows(c, ahead, t, b):
        if b == blocks - 1:
            return pltpu.roll(read(c, ahead, t, b), TILE - 1, 0)
        return ref[c, slot + ahead, t, pl.ds(b * TILE + 1, TILE)]

    def behind_rows(c, ahead, t, b):
        if b == 0:
            return pltpu.roll(read(c, ahead, t, b), 1, 0)
        return ref[c, slot + ahead, t, pl.ds(b * TILE - 1, TILE)]

    return read, ahead_rows, behind_rows


def magnetic_step(e, g, first, count, width, store):
    tiles, blocks = e.shape[2], e.shape[3] // TILE
    unroll = planes_at_once(count)

    def step(number, _):
        slot = first + number * unroll
        read, ahead_rows, _ = reader(e, slot)
        old, _, _ = reader(g, slot)
        results = {}
        for k in range(unroll):
            for b in range(blocks):
                y_x = ahead_lanes([read(1, k, t, b) for t in range(tiles)])
                z_x = ahead_lanes([read(2, k, t, b) for t in range(tiles)])
                for t in range(width):
                    ex, ey, ez = (read(c, k, t, b) for c in range(3))
                    curl = (
                        (ahead_rows(2, k, t, b) - ez) - (read(1, k + 1, t, b) - ey),
                        (read(0, k + 1, t, b) - ex) - (z_x[t] - ez),
                        (y_x[t] - ey) - (ahead_rows(0, k, t, b) - ex),
                    )
                    for c in range(3):
                        results[c, k, t, b] = old(c, k, t, b) + curl[c]
        store(slot, results)
        return 0

    lax.fori_loop(0, count // unroll, step, 0)


def dual_kernel(third_e, dual_g, dual_out):
    _, depth, rows, cols = dual_out.shape
    own, blocks = cols // LANES, rows // TILE + 1

    def store(slot, results):
        for c, k, t, b in results:
            if b == 0:
                values = gather([results[c, k, t, n] for n in range(blocks)])
                for n, value in enumerate(values):
                    where = (c, slot + k - BEFORE, rows_at(n), pl.ds(t * LANES, LANES))
                    dual_out[where] = value * COURANT

    magnetic_step(third_e, dual_g, BEFORE, depth, own, store)


def row_kernel(inverse, ya, yb_low, yb_high, placer, *state):
    state = state[5:]
    odd_y = place_on("gy")[1]
    own = ya.shape[2] // LANES
    height = state[0].shape[3]
    below, above = pl.ds(0, SHIFT), pl.ds(height - SHIFT, SHIFT)
    at_once = 4

    def place(array, start):
        def step(number, _):
            results = []
            for k in range(at_once):
                z = number * at_once + k
                arrived = jnp.concatenate([ya[start + z], array[z]], axis=0).astype(BF16)
                results.append(jnp.dot(placer[odd_y], arrived, preferred_element_type=F32))
            for k, halos in enumerate(results):
                z = number * at_once + k + start
                for c in range(COUNT):
                    for t in range(own):
                        halo = lane_tile(halos[c * TILE:(c + 1) * TILE], t)
                        if c == KAPPA:
                            halo = weight(halo, inverse)
                        at = (c % 3, z + BEFORE, t)
                        state[c // 3][(*at, below)] = halo[:SHIFT]
                        state[c // 3][(*at, above)] = halo[SHIFT:]
            return 0

        lax.fori_loop(0, array.shape[0] // at_once, step, 0)

    place(yb_low, 0)
    place(yb_high, yb_low.shape[0])


def window_kernel(x_messages, inverse, height, *others):
    corner_a, corner_b, corner_placing, table = others[:4]
    grad_out, forward_e, forward_g, dual_e, dual_g, factor, third_e, second_e = others[9:]
    rows, cols = height.shape
    depth = factor.shape[1] - BEFORE - AFTER
    own = cols // LANES
    tiles = own + 1
    blocks = rows // TILE + 1
    (at_x, odd_x), (at_y, odd_y), (at_z, odd_z) = (place_on(axis) for axis in ("gx", "gy", "gz"))
    start_z = at_z * depth
    row = row_of((TILE, LANES))
    lane = lane_of((TILE, LANES))
    zero = jnp.zeros((TILE, LANES), F32)
    state = (forward_e, forward_g, dual_e, dual_g, factor)
    below, above = pl.ds(0, SHIFT), pl.ds(blocks * TILE - SHIFT, SHIFT)

    for t in range(tiles):
        for b in range(blocks):
            for c in range(3):
                second_e[c, depth + BEFORE, t, rows_at(b)] = zero
                third_e[c, depth + BEFORE, t, rows_at(b)] = zero

    corner_tiles = LAYERS * WIDE // TILE
    groups = depth // TILE
    begin_halo = jnp.where(odd_z == 1, BEFORE - WIDE, BEFORE + depth)
    halo_group = jnp.where(odd_z == 1, groups - 1, 0)
    at = own * corner_tiles
    wides = []
    for count in [TILE] * x_messages + [WIDE] * x_messages:
        parts = [corner_a[at + k] + corner_b[at + k] for k in range(count)]
        wides.append(jnp.concatenate(parts, axis=0).astype(BF16))
        at += count
    for c in range(COUNT):
        ref, to = state[c // 3], c % 3
        for group in range(groups + 1):
            if group < groups:
                found = columns_of(table, odd_x, c, group, wides[:x_messages], inverse)
                slots = pl.ds(BEFORE + group * TILE, TILE)
            else:
                found = columns_of(table, odd_x, c, halo_group, wides[x_messages:], inverse)
                slots = pl.ds(begin_halo, WIDE)
            found = found.reshape(-1, TILE, LANES)
            ref[to, slots, own, below] = found[:, :SHIFT]
            ref[to, slots, own, above] = found[:, SHIFT:]

    group = LANES // rows
    group_tiles = group * WIDE // TILE
    plane_halos = []
    for n in range(LAYERS // group):
        arrived = jnp.concatenate([
            jnp.concatenate([ref[t * corner_tiles + k] for t in range(own)], axis=1)
            for ref in (corner_a, corner_b) for k in range(n * group_tiles, (n + 1) * group_tiles)
        ], axis=0).astype(BF16)
        placed = jnp.dot(corner_placing[odd_y], arrived, preferred_element_type=F32)
        plane_halos += [placed[k * TILE:(k + 1) * TILE] for k in range(group)]

    def halo_planes(layers):
        for n, (c, _, position) in enumerate(layers):
            for t in range(own):
                halo = lane_tile(plane_halos[n], t) * SCALE[c]
                if c == KAPPA:
                    halo = weight(halo, inverse)
                at = (c % 3, position + BEFORE, t)
                state[c // 3][(*at, below)] = halo[:SHIFT]
                state[c // 3][(*at, above)] = halo[SHIFT:]

    @pl.when(odd_z == 0)
    def _():
        halo_planes(layers_to_previous(depth))

    @pl.when(odd_z == 1)
    def _():
        halo_planes(layers_to_next(depth))

    keep_row = jnp.where((row < SHIFT) & (at_y == 0), 0.0, 1.0)
    keep_lane = jnp.where((lane >= LANES // 2) & (at_x == 0), 0.0, 1.0)

    def mask(value, t, b):
        if b == 0:
            value = value * keep_row
        if t == own:
            value = value * keep_lane
        return value

    def behind_lanes(parts):
        turned = [pltpu.roll(p, 1, 1) for p in parts]
        return [jnp.where(lane == 0, turned[(t - 1) % tiles], turned[t]) for t in range(tiles)]

    def begin(count):
        return first_slot(count, depth, odd_z)

    def magnetic(e, g, count):
        def store(slot, results):
            for (c, k, t, b), value in results.items():
                g[c, slot + k, t, rows_at(b)] = mask(value, t, b)

        magnetic_step(e, g, begin(count), count, tiles, store)

    def electric(e, g, to, count, partner=None, totals=()):
        unroll = planes_at_once(count)
        first = begin(count)

        def step(number, carry):
            carry = list(carry)
            slot = first + number * unroll
            read, _, behind_rows = reader(g, slot)
            old, _, _ = reader(e, slot)
            weights, _, _ = reader(factor, slot)
            results = {}
            for k in range(unroll):
                if partner is not None:
                    position = slot + k - BEFORE
                    inside = (position >= 0) & (position < depth)
                    position = jnp.where(inside, position + start_z, jnp.int32(2**30))
                for b in range(blocks):
                    y_x = behind_lanes([read(1, k, t, b) for t in range(tiles)])
                    z_x = behind_lanes([read(2, k, t, b) for t in range(tiles)])
                    for t in range(tiles):
                        gx, gy, gz = (read(c, k, t, b) for c in range(3))
                        curl = (
                            (gz - behind_rows(2, k, t, b)) - (gy - read(1, k - 1, t, b)),
                            (gx - read(0, k - 1, t, b)) - (gz - z_x[t]),
                            (gy - y_x[t]) - (gx - behind_rows(0, k, t, b)),
                        )
                        scale = weights(0, k, t, b)
                        product = None
                        for c in range(3):
                            value = old(c, k, t, b) - scale * curl[c]
                            results[c, k, t, b] = value
                            if partner is not None and t < own:
                                term = value * partner[c, slot + k, t, rows_at(b)]
                                product = term if product is None else product + term
                        if product is not None:
                            chosen = position < limits[t * blocks + b]
                            carry[t * blocks + b] += jnp.where(chosen, product, 0.0)
            for (c, k, t, b), value in results.items():
                to[c, slot + k, t, rows_at(b)] = value
            return tuple(carry)

        return lax.fori_loop(0, count // unroll, step, totals)

    def count(low, high):
        planes = depth + max(low, high)
        return planes if planes_at_once(planes) > 8 else planes + 1

    magnetic(dual_e, dual_g, count(2, 2))
    electric(dual_e, dual_g, second_e, count(1, 2))
    magnetic(second_e, dual_g, count(1, 1))
    electric(second_e, dual_g, third_e, count(0, 1))

    none = jnp.zeros((TILE, LANES), jnp.int32)
    limits = []
    for t in range(own):
        limits += spread(row_tiles(lane_tile(height[...], t)), none)
    totals = (zero,) * (own * blocks)
    magnetic(forward_e, forward_g, count(3, 2))
    totals = electric(forward_e, forward_g, forward_e, count(2, 2), third_e, totals)
    magnetic(forward_e, forward_g, count(2, 1))
    totals = electric(forward_e, forward_g, forward_e, count(1, 1), second_e, totals)
    magnetic(forward_e, forward_g, count(1, 0))
    totals = electric(forward_e, forward_g, forward_e, depth, dual_e, totals)
    for t in range(own):
        values = gather(list(totals[t * blocks:(t + 1) * blocks]))
        for b, value in enumerate(values):
            grad_out[rows_at(b), t * LANES:(t + 1) * LANES] = value


def corner_swap(array, axes, offsets):
    lengths = [lax.axis_size(a) for a in axes]
    pairs = [
        (i * lengths[1] + j, k * lengths[1] + l)
        for i, k in swap_pairs(lengths[0], offsets[0])
        for j, l in swap_pairs(lengths[1], offsets[1])
    ]
    return lax.ppermute(array, axes, pairs)


def local(forward_e, forward_h, adjoint_e, adjoint_h, material, inv_permittivity, height):
    depth, rows, cols = material.shape
    tiles = cols // LANES
    nx, nz = lax.axis_size("gx"), lax.axis_size("gz")
    assert nz == 2
    picker = jnp.asarray(row_picker(rows), BF16)
    placer = jnp.asarray(row_placer(rows), BF16)
    corner_picking = jnp.asarray(corner_picker(rows), BF16)
    corner_placing = jnp.asarray(corner_placer(rows), BF16)
    table = jnp.asarray(column_table(depth))
    vmem = pl.BlockSpec(memory_space=pltpu.VMEM)
    smem = pl.BlockSpec(memory_space=pltpu.SMEM)
    params = pltpu.CompilerParams(vmem_limit_bytes=24 * 1024 * 1024)
    anywhere = pl.BlockSpec(memory_space=pl.ANY)
    x_messages = 1 if nx == 2 else 2

    chunk = TILE
    x_shape = jax.ShapeDtypeStruct((chunk, rows, LANES), F32)
    xz_shape = jax.ShapeDtypeStruct((WIDE, rows, LANES), F32)
    y_shape = jax.ShapeDtypeStruct((depth, LAYERS, cols), F32)
    fields = (forward_e, forward_h, adjoint_e, adjoint_h, material)
    in_hbm = pl.BlockSpec(memory_space=pltpu.HBM)
    half_shape = jax.ShapeDtypeStruct((depth // 2, LAYERS, cols), F32)
    packed = pl.pallas_call(
        functools.partial(pack_kernel, x_messages),
        out_shape=[pltpu.VMEM(f.shape, f.dtype) for f in fields]
        + [x_shape] * x_messages + [xz_shape] * x_messages
        + [jax.ShapeDtypeStruct((LAYERS, rows, cols), F32), y_shape, half_shape, half_shape],
        in_specs=[in_hbm] * 5 + [vmem] * 2,
        out_specs=[vmem] * (2 * x_messages + 9),
        scratch_shapes=[pltpu.SemaphoreType.DMA((depth // TILE, COUNT))],
        compiler_params=pltpu.CompilerParams(vmem_limit_bytes=60 * 1024 * 1024),
        name="pack",
    )(*fields, picker, table)
    fields, packed = packed[:5], packed[5:]
    z_message, ya, yb_low, yb_high = packed[2 * x_messages:]
    ya = swap(ya, "gy", 0)
    zr = swap(z_message, "gz", 0)
    yb_low = swap(yb_low, "gy", 1)
    yb_high = swap(yb_high, "gy", 1)
    xp = [swap(packed[n], "gx", n) for n in range(x_messages)]
    xz = [corner_swap(packed[x_messages + n], ("gx", "gz"), (n, 0)) for n in range(x_messages)]

    block = (BEFORE + depth + AFTER, tiles + 1, (rows // TILE + 1) * TILE, LANES)
    state_shapes = [pltpu.VMEM((3,) + block, F32)] * 4 + [pltpu.VMEM((1,) + block, F32)]
    state = pl.pallas_call(
        prepare_kernel,
        out_shape=state_shapes,
        in_specs=[smem] + [vmem] * 5,
        out_specs=[vmem] * 5,
        compiler_params=params,
        name="prepare",
    )(inv_permittivity, *fields)

    corner_tiles = LAYERS * WIDE // TILE * tiles + x_messages * (chunk + WIDE)
    corner_shape = jax.ShapeDtypeStruct((corner_tiles, TILE, LANES), F32)
    corner_a, corner_b = pl.pallas_call(
        functools.partial(corner_kernel, x_messages),
        out_shape=[corner_shape, corner_shape],
        in_specs=[vmem] * (2 * x_messages + 2) + [anywhere],
        out_specs=[vmem] * 2,
        compiler_params=params,
        name="corners",
    )(*xp, *xz, zr, corner_picking, state[4])
    corner_b = swap(corner_b, "gy", 1)
    corner_a = swap(corner_a, "gy", 0)

    operands = (inv_permittivity, *xp, *xz, zr, table)
    state = pl.pallas_call(
        functools.partial(plane_kernel, x_messages),
        out_shape=state_shapes,
        in_specs=[smem] + [vmem] * (len(operands) + 4),
        out_specs=[vmem] * 5,
        input_output_aliases={len(operands) + n: n for n in range(5)},
        compiler_params=params,
        name="planes",
    )(*operands, *state)

    operands = (inv_permittivity, ya, yb_low, yb_high, placer)
    state = pl.pallas_call(
        row_kernel,
        out_shape=state_shapes,
        in_specs=[smem] + [vmem] * (len(operands) + 4),
        out_specs=[vmem] * 5,
        input_output_aliases={len(operands) + n: n for n in range(5)},
        compiler_params=params,
        name="rows",
    )(*operands, *state)

    operands = (inv_permittivity, height, corner_a, corner_b, corner_placing, table)
    results = pl.pallas_call(
        functools.partial(window_kernel, x_messages),
        out_shape=[jax.ShapeDtypeStruct((rows, cols), F32), *state_shapes, state_shapes[0]],
        in_specs=[smem] + [vmem] * (len(operands) + 4),
        out_specs=[vmem] * 7,
        input_output_aliases={len(operands) + n: 1 + n for n in range(5)},
        scratch_shapes=[pltpu.VMEM((3,) + block, F32)],
        compiler_params=params,
        name="window",
    )(*operands, *state)
    grad, dual_g, third_e = results[0], results[4], results[6]
    dual = pl.pallas_call(
        dual_kernel,
        out_shape=jax.ShapeDtypeStruct((3, depth, rows, cols), F32),
        in_specs=[vmem] * 2,
        out_specs=vmem,
        compiler_params=params,
        name="dual",
    )(third_e, dual_g)
    return grad + swap(grad, "gz", 0), dual


def solution(mesh):
    fields = P(None, "gz", "gy", "gx")
    return jax.shard_map(
        local,
        mesh=mesh,
        in_specs=(fields, fields, fields, fields, P("gz", "gy", "gx"), P(), P("gy", "gx")),
        out_specs=(P("gy", "gx"), fields),
        check_vma=False,
    )
```

```python
import functools

import jax
import jax.numpy as jnp
import numpy as np
from jax import lax
from jax.experimental import pallas as pl
from jax.experimental.pallas import tpu as pltpu
from jax.sharding import PartitionSpec as P

STEPS = 3
COURANT = 0.5
LANES = 128
TILE = 8
WIDE = 3
BEFORE = 5
AFTER = 5
SHIFT = 4
COUNT = 13
FE, FH, AE, AH, KAPPA = 0, 3, 6, 9, 12
LOW_DEPTH = [3] * 3 + [3] * 3 + [2] * 3 + [2] * 3 + [2]
HIGH_DEPTH = [3] * 3 + [2] * 3 + [3] * 3 + [2] * 3 + [2]
LAYERS = sum(LOW_DEPTH)
SCALE = [1.0] * 3 + [-1.0 / COURANT] * 3 + [1.0] * 3 + [1.0 / COURANT] * 3 + [1.0]
F32 = jnp.float32
BF16 = jnp.bfloat16


def layers_to_next(length):
    return [(c, length - d + k, k - d) for c, d in enumerate(LOW_DEPTH) for k in range(d)]


def layers_to_previous(length):
    return [(c, k, length + k) for c, d in enumerate(HIGH_DEPTH) for k in range(d)]


def swap_pairs(length, offset):
    pairs = []
    for i in range(offset, length - 1, 2):
        pairs += [(i, i + 1), (i + 1, i)]
    return pairs


def swap(array, axis, offset):
    return lax.ppermute(array, axis, swap_pairs(lax.axis_size(axis), offset))


def two_ways(rows_in, to_next, to_previous):
    first, second = np.zeros((2, len(to_next), rows_in), np.float32)
    for n, index in enumerate(to_next):
        first[n, index] = 1
    for n, index in enumerate(to_previous):
        second[n, index] = 1
    return np.stack([np.concatenate([first, second]), np.concatenate([second, first])])


def row_picker(rows):
    return two_ways(
        COUNT * rows,
        [c * rows + own for c, own, _ in layers_to_next(rows)],
        [c * rows + own for c, own, _ in layers_to_previous(rows)],
    )


def corner_picker(rows):
    group = LANES // rows
    return two_ways(
        LANES,
        [n * rows + rows - WIDE + k for n in range(group) for k in range(WIDE)],
        [n * rows + k for n in range(group) for k in range(WIDE)],
    )


def ways_back(rows_out, low, high):
    first = np.zeros((rows_out, len(low)), np.float32)
    second = np.zeros((rows_out, len(high)), np.float32)
    for n, (index, value) in enumerate(low):
        first[index, n] = value
    for n, (index, value) in enumerate(high):
        second[index, n] = value
    return np.stack([np.concatenate([second, first], 1), np.concatenate([first, second], 1)])


def row_placer(rows):
    low = [(c * TILE + there + SHIFT, SCALE[c]) for c, _, there in layers_to_next(rows)]
    high = [(c * TILE + there - rows + SHIFT, SCALE[c]) for c, _, there in layers_to_previous(rows)]
    return ways_back(COUNT * TILE, low, high)


def corner_placer(rows):
    group = LANES // rows
    low = [(n * TILE + SHIFT - WIDE + k, 1) for n in range(group) for k in range(WIDE)]
    high = [(n * TILE + SHIFT + k, 1) for n in range(group) for k in range(WIDE)]
    return ways_back(group * TILE, low, high)


def column_table(depth):
    groups = depth // TILE
    assert groups * LAYERS <= LANES
    table = np.full((2, TILE, LANES), -1, np.int32)
    for way, layers in enumerate((layers_to_next(LANES), layers_to_previous(0))):
        for g in range(groups):
            for n, (c, own, there) in enumerate(layers):
                lane = g * LAYERS + n
                table[way, :4, lane] = c, own, there % LANES, g
    return table


def lane_of(shape):
    return lax.broadcasted_iota(jnp.int32, shape, len(shape) - 1)


def row_of(shape):
    return lax.broadcasted_iota(jnp.int32, shape, len(shape) - 2)


def own_field(refs, c, z):
    fe, fh, ae, ah, material = refs
    if c == KAPPA:
        return (material[z] + 1).astype(F32).astype(BF16)
    return (fe, fh, ae, ah)[c // 3][c % 3, z]


def place_on(axis):
    return lax.axis_index(axis), lax.rem(lax.axis_index(axis), 2)


def pack_kernel(x_messages, *refs):
    whole, (picker, table), refs = refs[:5], refs[5:7], refs[7:]
    fields, refs = refs[:5], refs[5:]
    x_out, xz_out = refs[:x_messages], refs[x_messages:2 * x_messages]
    z_out, ya_out, yb_low_out, yb_high_out, arrived = refs[2 * x_messages:]
    depth, rows, cols = fields[4].shape
    odd_x, odd_y, odd_z = (place_on(axis)[1] for axis in ("gx", "gy", "gz"))
    groups = depth // TILE

    copies = []
    for group in range(groups):
        planes = pl.ds(group * TILE, TILE)
        parts = [(n, c, planes) for n in range(4) for c in range(3)] + [(4, planes)]
        copies.append([
            pltpu.make_async_copy(
                whole[n].at[at], fields[n].at[at], arrived.at[group, number]
            )
            for number, (n, *at) in enumerate((p[0], *p[1:]) for p in parts)
            for at in [tuple(at)]
        ])
    for group in copies:
        for copy in group:
            copy.start()

    totals = [jnp.zeros((TILE * rows, LANES), F32)] * x_messages
    for group in range(groups):
        for copy in copies[group]:
            copy.wait()
        for z in range(group * TILE, (group + 1) * TILE):
            stacked = jnp.concatenate([own_field(fields, c, z) for c in range(COUNT)], axis=0)
            picked = jnp.dot(picker[odd_y], stacked, preferred_element_type=F32)
            ya_out[z] = picked[:LAYERS]
            half = yb_low_out.shape[0]
            if z < half:
                yb_low_out[z] = picked[LAYERS:]
            else:
                yb_high_out[z - half] = picked[LAYERS:]

        for number in range(x_messages):
            way = odd_x ^ number
            offset = pl.multiple_of((1 - way) * (cols - LANES), LANES)
            of_field, of_lane, of_group = (table[way, k:k + 1, :] for k in (0, 1, 3))
            chosen = (row_of((LANES, LANES)) == of_lane) & (of_group == group)
            planes = pl.ds(group * TILE, TILE)
            for c in range(COUNT):
                if c == KAPPA:
                    part = fields[4][planes, :, pl.ds(offset, LANES)]
                    part = (part + 1).astype(F32).astype(BF16)
                else:
                    part = fields[c // 3][c % 3, planes, :, pl.ds(offset, LANES)]
                matrix = jnp.where(chosen & (of_field == c), 1.0, 0.0).astype(BF16)
                totals[number] += jnp.dot(
                    part.reshape(TILE * rows, LANES), matrix, preferred_element_type=F32
                )

    edge = jnp.where(odd_z == 0, TILE - WIDE, 0)
    for total, out, part in zip(totals, x_out, xz_out):
        out[...] = total.reshape(TILE, rows, LANES)
        part[...] = out[pl.ds(edge, WIDE)]

    def edges(layers):
        for n, (c, own, _) in enumerate(layers):
            z_out[n] = own_field(fields, c, own).astype(F32)

    @pl.when(odd_z == 0)
    def _():
        edges(layers_to_next(depth))

    @pl.when(odd_z == 1)
    def _():
        edges(layers_to_previous(depth))


def edge_rows(array, to_next):
    rows = array.shape[0]
    row = row_of((TILE, LANES))
    last = pltpu.roll(array[rows - TILE:], SHIFT, 0)
    first = pltpu.roll(array[:TILE], SHIFT, 0)
    last = jnp.where((row >= SHIFT - WIDE) & (row < SHIFT), last, 0.0)
    first = jnp.where((row >= SHIFT) & (row < SHIFT + WIDE), first, 0.0)
    return jnp.where(to_next == 1, last, first)


def corner_kernel(x_messages, *refs):
    arrays = refs[:2 * x_messages]
    zr, picker, _, a_out, b_out = refs[2 * x_messages:]
    _, rows, cols = zr.shape
    odd_y = place_on("gy")[1]
    arrived = zr[...].reshape(LAYERS * rows, cols).astype(BF16)
    picked = [
        jnp.dot(picker[odd_y], arrived[n:n + LANES], preferred_element_type=F32)
        for n in range(0, LAYERS * rows, LANES)
    ]
    count = picker.shape[1] // 2
    for message, out in ((0, a_out), (1, b_out)):
        at = 0
        for t in range(cols // LANES):
            for group in picked:
                for n in range(message * count, (message + 1) * count, TILE):
                    out[at] = lane_tile(group[n:n + TILE], t)
                    at += 1
        for array in arrays:
            for k in range(array.shape[0]):
                out[at + k] = edge_rows(array[k], 1 - (odd_y ^ message))
            at += array.shape[0]


def spread(tiles, halo):
    low = row_of((TILE, LANES)) < SHIFT
    turned = [pltpu.roll(t, SHIFT, 0) for t in tiles]
    out = [jnp.where(low, halo, turned[0])]
    for before, after in zip(turned, turned[1:]):
        out.append(jnp.where(low, before, after))
    out.append(jnp.where(low, turned[-1], halo))
    return out


def gather(tiles):
    low = row_of((TILE, LANES)) < SHIFT
    turned = [pltpu.roll(t, SHIFT, 0) for t in tiles]
    return [jnp.where(low, before, after) for before, after in zip(turned, turned[1:])]


def planes_at_once(count):
    return max(n for n in range(1, 18) if count % n == 0)


def lane_tile(array, t):
    return array[:, t * LANES:(t + 1) * LANES]


def row_tiles(array):
    return [array[b:b + TILE] for b in range(0, array.shape[0], TILE)]


def rows_at(b):
    return pl.ds(b * TILE, TILE)


def weight(number, inverse):
    value = jnp.zeros(number.shape, F32)
    for m in range(inverse.shape[0]):
        value = jnp.where(number == m + 1, inverse[m] * (COURANT * COURANT), value)
    return value


def arrange(c, own_tiles, halo, inverse):
    if c == KAPPA:
        own_tiles = [weight(p, inverse) for p in own_tiles]
        halo = weight(halo, inverse)
    elif SCALE[c] != 1.0:
        own_tiles = [p * SCALE[c] for p in own_tiles]
        halo = halo * SCALE[c]
    return spread(own_tiles, halo)


def prepare_kernel(inverse, fe, fh, ae, ah, material, _, *state):
    depth, _, cols = material.shape
    refs = (fe, fh, ae, ah, material)
    zero = jnp.zeros((TILE, LANES), F32)

    def planes(step, _):
        for k in range(4):
            z = step * 4 + k
            for c in range(COUNT):
                whole = own_field(refs, c, z).astype(F32)
                for t in range(cols // LANES):
                    parts = arrange(c, row_tiles(lane_tile(whole, t)), zero, inverse)
                    for b, part in enumerate(parts):
                        state[c // 3][c % 3, BEFORE + z, t, rows_at(b)] = part
        return 0

    lax.fori_loop(0, depth // 4, planes, 0)


def column_matrix(table, odd_x, number, c, group):
    way = 1 - (odd_x ^ number)
    of_field, of_target, of_group = (table[way, k:k + 1, :] for k in (0, 2, 3))
    chosen = (of_field == c) & (of_group == group) & (of_target == row_of((LANES, LANES)))
    return jnp.where(chosen, SCALE[c], 0.0).astype(BF16)


def columns_of(table, odd_x, c, group, arrays, inverse):
    total = None
    for number, array in enumerate(arrays):
        part = lax.dot_general(
            array, column_matrix(table, odd_x, number, c, group), (((1,), (1,)), ((), ())),
            preferred_element_type=F32,
        )
        total = part if total is None else total + part
    return weight(total, inverse) if c == KAPPA else total


def plane_kernel(x_messages, inverse, *others):
    xp, xz = others[:x_messages], others[x_messages:2 * x_messages]
    zr, table = others[2 * x_messages:2 * x_messages + 2]
    state = others[2 * x_messages + 7:]
    _, rows, cols = zr.shape
    own = cols // LANES
    blocks = rows // TILE + 1
    depth = state[0].shape[1] - BEFORE - AFTER
    odd_x, odd_z = (place_on(axis)[1] for axis in ("gx", "gz"))
    zero = jnp.zeros((TILE, LANES), F32)

    for t in range(own + 1):
        for b in range(blocks):
            for c in range(3):
                for ref, slot in zip(state, (depth + BEFORE, BEFORE - 1) * 2):
                    ref[c, slot, t, rows_at(b)] = zero

    groups = depth // TILE
    begin_halo = jnp.where(odd_z == 1, BEFORE - WIDE, BEFORE + depth)
    halo_group = jnp.where(odd_z == 1, groups - 1, 0)
    wides = []
    for array in (*xp, *xz):
        parts = []
        for k in range(array.shape[0]):
            parts += spread(row_tiles(array[k]), zero)
        wides.append(jnp.concatenate(parts, axis=0).astype(BF16))
    for c in range(COUNT):
        ref, to = state[c // 3], c % 3
        for group in range(groups):
            found = columns_of(table, odd_x, c, group, wides[:x_messages], inverse)
            found = found.reshape(TILE, blocks * TILE, LANES)
            ref[to, pl.ds(BEFORE + group * TILE, TILE), own] = found
        found = columns_of(table, odd_x, c, halo_group, wides[x_messages:], inverse)
        ref[to, pl.ds(begin_halo, WIDE), own] = found.reshape(WIDE, blocks * TILE, LANES)

    def halo_planes(layers):
        for n, (c, _, position) in enumerate(layers):
            for t in range(own):
                parts = arrange(c, row_tiles(lane_tile(zr[n], t)), zero, inverse)
                for b, part in enumerate(parts):
                    state[c // 3][c % 3, position + BEFORE, t, rows_at(b)] = part

    @pl.when(odd_z == 0)
    def _():
        halo_planes(layers_to_previous(depth))

    @pl.when(odd_z == 1)
    def _():
        halo_planes(layers_to_next(depth))


def first_slot(count, depth, odd_z):
    return BEFORE + jnp.where(odd_z == 1, depth - count, 0)


def ahead_lanes(parts):
    lane = lane_of((TILE, LANES))
    turned = [pltpu.roll(p, LANES - 1, 1) for p in parts]
    after = turned[1:] + turned[:1]
    return [jnp.where(lane == LANES - 1, a, t) for a, t in zip(after, turned)]


def reader(ref, slot):
    blocks = ref.shape[3] // TILE
    seen = {}

    def read(c, ahead, t, b):
        if (c, ahead, t, b) not in seen:
            seen[c, ahead, t, b] = ref[c, slot + ahead, t, rows_at(b)]
        return seen[c, ahead, t, b]

    def ahead_rows(c, ahead, t, b):
        if b == blocks - 1:
            return pltpu.roll(read(c, ahead, t, b), TILE - 1, 0)
        return ref[c, slot + ahead, t, pl.ds(b * TILE + 1, TILE)]

    def behind_rows(c, ahead, t, b):
        if b == 0:
            return pltpu.roll(read(c, ahead, t, b), 1, 0)
        return ref[c, slot + ahead, t, pl.ds(b * TILE - 1, TILE)]

    return read, ahead_rows, behind_rows


def magnetic_step(e, g, first, count, width, store):
    tiles, blocks = e.shape[2], e.shape[3] // TILE
    unroll = planes_at_once(count)

    def step(number, _):
        slot = first + number * unroll
        read, ahead_rows, _ = reader(e, slot)
        old, _, _ = reader(g, slot)
        results = {}
        for k in range(unroll):
            for b in range(blocks):
                y_x = ahead_lanes([read(1, k, t, b) for t in range(tiles)])
                z_x = ahead_lanes([read(2, k, t, b) for t in range(tiles)])
                for t in range(width):
                    ex, ey, ez = (read(c, k, t, b) for c in range(3))
                    curl = (
                        (ahead_rows(2, k, t, b) - ez) - (read(1, k + 1, t, b) - ey),
                        (read(0, k + 1, t, b) - ex) - (z_x[t] - ez),
                        (y_x[t] - ey) - (ahead_rows(0, k, t, b) - ex),
                    )
                    for c in range(3):
                        results[c, k, t, b] = old(c, k, t, b) + curl[c]
        store(slot, results)
        return 0

    lax.fori_loop(0, count // unroll, step, 0)


def dual_kernel(third_e, dual_g, dual_out):
    _, depth, rows, cols = dual_out.shape
    own, blocks = cols // LANES, rows // TILE + 1

    def store(slot, results):
        for c, k, t, b in results:
            if b == 0:
                values = gather([results[c, k, t, n] for n in range(blocks)])
                for n, value in enumerate(values):
                    where = (c, slot + k - BEFORE, rows_at(n), pl.ds(t * LANES, LANES))
                    dual_out[where] = value * COURANT

    magnetic_step(third_e, dual_g, BEFORE, depth, own, store)


def row_kernel(inverse, ya, yb_low, yb_high, placer, *state):
    state = state[5:]
    odd_y = place_on("gy")[1]
    own = ya.shape[2] // LANES
    height = state[0].shape[3]
    below, above = pl.ds(0, SHIFT), pl.ds(height - SHIFT, SHIFT)
    at_once = 4

    def place(array, start):
        def step(number, _):
            results = []
            for k in range(at_once):
                z = number * at_once + k
                arrived = jnp.concatenate([ya[start + z], array[z]], axis=0).astype(BF16)
                results.append(jnp.dot(placer[odd_y], arrived, preferred_element_type=F32))
            for k, halos in enumerate(results):
                z = number * at_once + k + start
                for c in range(COUNT):
                    for t in range(own):
                        halo = lane_tile(halos[c * TILE:(c + 1) * TILE], t)
                        if c == KAPPA:
                            halo = weight(halo, inverse)
                        at = (c % 3, z + BEFORE, t)
                        state[c // 3][(*at, below)] = halo[:SHIFT]
                        state[c // 3][(*at, above)] = halo[SHIFT:]
            return 0

        lax.fori_loop(0, array.shape[0] // at_once, step, 0)

    place(yb_low, 0)
    place(yb_high, yb_low.shape[0])


def window_kernel(x_messages, inverse, height, *others):
    corner_a, corner_b, corner_placing, table = others[:4]
    grad_out, forward_e, forward_g, dual_e, dual_g, factor, third_e, second_e = others[9:]
    rows, cols = height.shape
    depth = factor.shape[1] - BEFORE - AFTER
    own = cols // LANES
    tiles = own + 1
    blocks = rows // TILE + 1
    (at_x, odd_x), (at_y, odd_y), (at_z, odd_z) = (place_on(axis) for axis in ("gx", "gy", "gz"))
    start_z = at_z * depth
    row = row_of((TILE, LANES))
    lane = lane_of((TILE, LANES))
    zero = jnp.zeros((TILE, LANES), F32)
    state = (forward_e, forward_g, dual_e, dual_g, factor)
    below, above = pl.ds(0, SHIFT), pl.ds(blocks * TILE - SHIFT, SHIFT)

    for t in range(tiles):
        for b in range(blocks):
            for c in range(3):
                second_e[c, depth + BEFORE, t, rows_at(b)] = zero
                third_e[c, depth + BEFORE, t, rows_at(b)] = zero

    corner_tiles = LAYERS * WIDE // TILE
    groups = depth // TILE
    begin_halo = jnp.where(odd_z == 1, BEFORE - WIDE, BEFORE + depth)
    halo_group = jnp.where(odd_z == 1, groups - 1, 0)
    at = own * corner_tiles
    wides = []
    for count in [TILE] * x_messages + [WIDE] * x_messages:
        parts = [corner_a[at + k] + corner_b[at + k] for k in range(count)]
        wides.append(jnp.concatenate(parts, axis=0).astype(BF16))
        at += count
    for c in range(COUNT):
        ref, to = state[c // 3], c % 3
        for group in range(groups + 1):
            if group < groups:
                found = columns_of(table, odd_x, c, group, wides[:x_messages], inverse)
                slots = pl.ds(BEFORE + group * TILE, TILE)
            else:
                found = columns_of(table, odd_x, c, halo_group, wides[x_messages:], inverse)
                slots = pl.ds(begin_halo, WIDE)
            found = found.reshape(-1, TILE, LANES)
            ref[to, slots, own, below] = found[:, :SHIFT]
            ref[to, slots, own, above] = found[:, SHIFT:]

    group = LANES // rows
    group_tiles = group * WIDE // TILE
    plane_halos = []
    for n in range(LAYERS // group):
        arrived = jnp.concatenate([
            jnp.concatenate([ref[t * corner_tiles + k] for t in range(own)], axis=1)
            for ref in (corner_a, corner_b) for k in range(n * group_tiles, (n + 1) * group_tiles)
        ], axis=0).astype(BF16)
        placed = jnp.dot(corner_placing[odd_y], arrived, preferred_element_type=F32)
        plane_halos += [placed[k * TILE:(k + 1) * TILE] for k in range(group)]

    def halo_planes(layers):
        for n, (c, _, position) in enumerate(layers):
            for t in range(own):
                halo = lane_tile(plane_halos[n], t) * SCALE[c]
                if c == KAPPA:
                    halo = weight(halo, inverse)
                at = (c % 3, position + BEFORE, t)
                state[c // 3][(*at, below)] = halo[:SHIFT]
                state[c // 3][(*at, above)] = halo[SHIFT:]

    @pl.when(odd_z == 0)
    def _():
        halo_planes(layers_to_previous(depth))

    @pl.when(odd_z == 1)
    def _():
        halo_planes(layers_to_next(depth))

    keep_row = jnp.where((row < SHIFT) & (at_y == 0), 0.0, 1.0)
    keep_lane = jnp.where((lane >= LANES // 2) & (at_x == 0), 0.0, 1.0)

    def mask(value, t, b):
        if b == 0:
            value = value * keep_row
        if t == own:
            value = value * keep_lane
        return value

    def behind_lanes(parts):
        turned = [pltpu.roll(p, 1, 1) for p in parts]
        return [jnp.where(lane == 0, turned[(t - 1) % tiles], turned[t]) for t in range(tiles)]

    def begin(count):
        return first_slot(count, depth, odd_z)

    def magnetic(e, g, count):
        def store(slot, results):
            for (c, k, t, b), value in results.items():
                g[c, slot + k, t, rows_at(b)] = mask(value, t, b)

        magnetic_step(e, g, begin(count), count, tiles, store)

    def electric(e, g, to, count, partner=None, totals=()):
        unroll = planes_at_once(count)
        first = begin(count)

        def step(number, carry):
            carry = list(carry)
            slot = first + number * unroll
            read, _, behind_rows = reader(g, slot)
            old, _, _ = reader(e, slot)
            weights, _, _ = reader(factor, slot)
            results = {}
            for k in range(unroll):
                if partner is not None:
                    position = slot + k - BEFORE
                    inside = (position >= 0) & (position < depth)
                    position = jnp.where(inside, position + start_z, jnp.int32(2**30))
                for b in range(blocks):
                    y_x = behind_lanes([read(1, k, t, b) for t in range(tiles)])
                    z_x = behind_lanes([read(2, k, t, b) for t in range(tiles)])
                    for t in range(tiles):
                        gx, gy, gz = (read(c, k, t, b) for c in range(3))
                        curl = (
                            (gz - behind_rows(2, k, t, b)) - (gy - read(1, k - 1, t, b)),
                            (gx - read(0, k - 1, t, b)) - (gz - z_x[t]),
                            (gy - y_x[t]) - (gx - behind_rows(0, k, t, b)),
                        )
                        scale = weights(0, k, t, b)
                        product = None
                        for c in range(3):
                            value = old(c, k, t, b) - scale * curl[c]
                            results[c, k, t, b] = value
                            if partner is not None and t < own:
                                term = value * partner[c, slot + k, t, rows_at(b)]
                                product = term if product is None else product + term
                        if product is not None:
                            chosen = position < limits[t * blocks + b]
                            carry[t * blocks + b] += jnp.where(chosen, product, 0.0)
            for (c, k, t, b), value in results.items():
                to[c, slot + k, t, rows_at(b)] = value
            return tuple(carry)

        return lax.fori_loop(0, count // unroll, step, totals)

    def count(low, high):
        planes = depth + max(low, high)
        return planes if planes_at_once(planes) > 8 else planes + 1

    magnetic(dual_e, dual_g, count(2, 2))
    electric(dual_e, dual_g, second_e, count(1, 2))
    magnetic(second_e, dual_g, count(1, 1))
    electric(second_e, dual_g, third_e, count(0, 1))

    none = jnp.zeros((TILE, LANES), jnp.int32)
    limits = []
    for t in range(own):
        limits += spread(row_tiles(lane_tile(height[...], t)), none)
    totals = (zero,) * (own * blocks)
    magnetic(forward_e, forward_g, count(3, 2))
    totals = electric(forward_e, forward_g, forward_e, count(2, 2), third_e, totals)
    magnetic(forward_e, forward_g, count(2, 1))
    totals = electric(forward_e, forward_g, forward_e, count(1, 1), second_e, totals)
    magnetic(forward_e, forward_g, count(1, 0))
    totals = electric(forward_e, forward_g, forward_e, depth, dual_e, totals)
    for t in range(own):
        values = gather(list(totals[t * blocks:(t + 1) * blocks]))
        for b, value in enumerate(values):
            grad_out[rows_at(b), t * LANES:(t + 1) * LANES] = value


def corner_swap(array, axes, offsets):
    lengths = [lax.axis_size(a) for a in axes]
    pairs = [
        (i * lengths[1] + j, k * lengths[1] + l)
        for i, k in swap_pairs(lengths[0], offsets[0])
        for j, l in swap_pairs(lengths[1], offsets[1])
    ]
    return lax.ppermute(array, axes, pairs)


def local(forward_e, forward_h, adjoint_e, adjoint_h, material, inv_permittivity, height):
    depth, rows, cols = material.shape
    tiles = cols // LANES
    nx, nz = lax.axis_size("gx"), lax.axis_size("gz")
    assert nz == 2
    picker = jnp.asarray(row_picker(rows), BF16)
    placer = jnp.asarray(row_placer(rows), BF16)
    corner_picking = jnp.asarray(corner_picker(rows), BF16)
    corner_placing = jnp.asarray(corner_placer(rows), BF16)
    table = jnp.asarray(column_table(depth))
    vmem = pl.BlockSpec(memory_space=pltpu.VMEM)
    smem = pl.BlockSpec(memory_space=pltpu.SMEM)
    params = pltpu.CompilerParams(vmem_limit_bytes=24 * 1024 * 1024)
    anywhere = pl.BlockSpec(memory_space=pl.ANY)
    x_messages = 1 if nx == 2 else 2

    chunk = TILE
    x_shape = pltpu.VMEM((chunk, rows, LANES), F32)
    xz_shape = pltpu.VMEM((WIDE, rows, LANES), F32)
    y_shape = pltpu.VMEM((depth, LAYERS, cols), F32)
    fields = (forward_e, forward_h, adjoint_e, adjoint_h, material)
    in_hbm = pl.BlockSpec(memory_space=pltpu.HBM)
    half_shape = pltpu.VMEM((depth // 2, LAYERS, cols), F32)
    packed = pl.pallas_call(
        functools.partial(pack_kernel, x_messages),
        out_shape=[pltpu.VMEM(f.shape, f.dtype) for f in fields]
        + [x_shape] * x_messages + [xz_shape] * x_messages
        + [pltpu.VMEM((LAYERS, rows, cols), F32), y_shape, half_shape, half_shape],
        in_specs=[in_hbm] * 5 + [vmem] * 2,
        out_specs=[vmem] * (2 * x_messages + 9),
        scratch_shapes=[pltpu.SemaphoreType.DMA((depth // TILE, COUNT))],
        compiler_params=pltpu.CompilerParams(vmem_limit_bytes=56 * 1024 * 1024),
        name="pack",
    )(*fields, picker, table)
    fields, packed = packed[:5], packed[5:]
    z_message, ya, yb_low, yb_high = packed[2 * x_messages:]
    ya = swap(ya, "gy", 0)
    zr = swap(z_message, "gz", 0)
    yb_low = swap(yb_low, "gy", 1)
    yb_high = swap(yb_high, "gy", 1)
    xp = [swap(packed[n], "gx", n) for n in range(x_messages)]
    xz = [corner_swap(packed[x_messages + n], ("gx", "gz"), (n, 0)) for n in range(x_messages)]

    block = (BEFORE + depth + AFTER, tiles + 1, (rows // TILE + 1) * TILE, LANES)
    state_shapes = [pltpu.VMEM((3,) + block, F32)] * 4 + [pltpu.VMEM((1,) + block, F32)]
    state = pl.pallas_call(
        prepare_kernel,
        out_shape=state_shapes,
        in_specs=[smem] + [vmem] * 5 + [anywhere],
        out_specs=[vmem] * 5,
        compiler_params=pltpu.CompilerParams(vmem_limit_bytes=8 * 1024 * 1024),
        name="prepare",
    )(inv_permittivity, *fields, ya)

    corner_tiles = LAYERS * WIDE // TILE * tiles + x_messages * (chunk + WIDE)
    corner_shape = jax.ShapeDtypeStruct((corner_tiles, TILE, LANES), F32)
    corner_a, corner_b = pl.pallas_call(
        functools.partial(corner_kernel, x_messages),
        out_shape=[corner_shape, corner_shape],
        in_specs=[vmem] * (2 * x_messages + 2) + [anywhere],
        out_specs=[vmem] * 2,
        compiler_params=pltpu.CompilerParams(vmem_limit_bytes=8 * 1024 * 1024),
        name="corners",
    )(*xp, *xz, zr, corner_picking, state[4])
    corner_b = swap(corner_b, "gy", 1)
    corner_a = swap(corner_a, "gy", 0)

    operands = (inv_permittivity, *xp, *xz, zr, table)
    state = pl.pallas_call(
        functools.partial(plane_kernel, x_messages),
        out_shape=state_shapes,
        in_specs=[smem] + [vmem] * (len(operands) + 4),
        out_specs=[vmem] * 5,
        input_output_aliases={len(operands) + n: n for n in range(5)},
        compiler_params=pltpu.CompilerParams(vmem_limit_bytes=8 * 1024 * 1024),
        name="planes",
    )(*operands, *state)

    operands = (inv_permittivity, ya, yb_low, yb_high, placer)
    state = pl.pallas_call(
        row_kernel,
        out_shape=state_shapes,
        in_specs=[smem] + [vmem] * (len(operands) + 4),
        out_specs=[vmem] * 5,
        input_output_aliases={len(operands) + n: n for n in range(5)},
        compiler_params=pltpu.CompilerParams(vmem_limit_bytes=8 * 1024 * 1024),
        name="rows",
    )(*operands, *state)

    operands = (inv_permittivity, height, corner_a, corner_b, corner_placing, table)
    results = pl.pallas_call(
        functools.partial(window_kernel, x_messages),
        out_shape=[jax.ShapeDtypeStruct((rows, cols), F32), *state_shapes, state_shapes[0]],
        in_specs=[smem] + [vmem] * (len(operands) + 4),
        out_specs=[vmem] * 7,
        input_output_aliases={len(operands) + n: 1 + n for n in range(5)},
        scratch_shapes=[pltpu.VMEM((3,) + block, F32)],
        compiler_params=pltpu.CompilerParams(vmem_limit_bytes=16 * 1024 * 1024),
        name="window",
    )(*operands, *state)
    grad, dual_g, third_e = results[0], results[4], results[6]
    dual = pl.pallas_call(
        dual_kernel,
        out_shape=jax.ShapeDtypeStruct((3, depth, rows, cols), F32),
        in_specs=[vmem] * 2,
        out_specs=vmem,
        compiler_params=pltpu.CompilerParams(vmem_limit_bytes=8 * 1024 * 1024),
        name="dual",
    )(third_e, dual_g)
    return grad + swap(grad, "gz", 0), dual


def solution(mesh):
    fields = P(None, "gz", "gy", "gx")
    return jax.shard_map(
        local,
        mesh=mesh,
        in_specs=(fields, fields, fields, fields, P("gz", "gy", "gx"), P(), P("gy", "gx")),
        out_specs=(P("gy", "gx"), fields),
        check_vma=False,
    )
```

```python
import functools

import jax
import jax.numpy as jnp
import numpy as np
from jax import lax
from jax.experimental import pallas as pl
from jax.experimental.pallas import tpu as pltpu
from jax.sharding import PartitionSpec as P

STEPS = 3
COURANT = 0.5
LANES = 128
TILE = 8
WIDE = 3
BEFORE = 5
AFTER = 5
SHIFT = 4
COUNT = 13
FE, FH, AE, AH, KAPPA = 0, 3, 6, 9, 12
LOW_DEPTH = [3] * 3 + [3] * 3 + [2] * 3 + [2] * 3 + [2]
HIGH_DEPTH = [3] * 3 + [2] * 3 + [3] * 3 + [2] * 3 + [2]
LAYERS = sum(LOW_DEPTH)
SCALE = [1.0] * 3 + [-1.0 / COURANT] * 3 + [1.0] * 3 + [1.0 / COURANT] * 3 + [1.0]
F32 = jnp.float32
BF16 = jnp.bfloat16


def layers_to_next(length):
    return [(c, length - d + k, k - d) for c, d in enumerate(LOW_DEPTH) for k in range(d)]


def layers_to_previous(length):
    return [(c, k, length + k) for c, d in enumerate(HIGH_DEPTH) for k in range(d)]


def planes_to_next(depth):
    return [e for e in layers_to_next(depth) if not (e[0] in (FH + 2, AH + 2) and -e[2] == LOW_DEPTH[e[0]])]


def planes_to_previous(depth):
    return [
        e for e in layers_to_previous(depth)
        if not (e[0] in (FE + 2, AE + 2) and e[1] == HIGH_DEPTH[e[0]] - 1)
    ]


def swap_pairs(length, offset):
    pairs = []
    for i in range(offset, length - 1, 2):
        pairs += [(i, i + 1), (i + 1, i)]
    return pairs


def swap(array, axis, offset):
    return lax.ppermute(array, axis, swap_pairs(lax.axis_size(axis), offset))


def two_ways(rows_in, to_next, to_previous):
    first, second = np.zeros((2, len(to_next), rows_in), np.float32)
    for n, index in enumerate(to_next):
        first[n, index] = 1
    for n, index in enumerate(to_previous):
        second[n, index] = 1
    return np.stack([np.concatenate([first, second]), np.concatenate([second, first])])


def row_picker(rows):
    return two_ways(
        COUNT * rows,
        [c * rows + own for c, own, _ in layers_to_next(rows)],
        [c * rows + own for c, own, _ in layers_to_previous(rows)],
    )


def corner_picker(rows):
    group = LANES // rows
    return two_ways(
        LANES,
        [n * rows + rows - WIDE + k for n in range(group) for k in range(WIDE)],
        [n * rows + k for n in range(group) for k in range(WIDE)],
    )


def ways_back(rows_out, low, high):
    first = np.zeros((rows_out, len(low)), np.float32)
    second = np.zeros((rows_out, len(high)), np.float32)
    for n, (index, value) in enumerate(low):
        first[index, n] = value
    for n, (index, value) in enumerate(high):
        second[index, n] = value
    return np.stack([np.concatenate([second, first], 1), np.concatenate([first, second], 1)])


def row_placer(rows):
    low = [(c * TILE + there + SHIFT, SCALE[c]) for c, _, there in layers_to_next(rows)]
    high = [(c * TILE + there - rows + SHIFT, SCALE[c]) for c, _, there in layers_to_previous(rows)]
    return ways_back(COUNT * TILE, low, high)


def corner_placer(rows):
    group = LANES // rows
    low = [(n * TILE + SHIFT - WIDE + k, 1) for n in range(group) for k in range(WIDE)]
    high = [(n * TILE + SHIFT + k, 1) for n in range(group) for k in range(WIDE)]
    return ways_back(group * TILE, low, high)


def column_table(depth):
    groups = depth // TILE
    assert groups * LAYERS <= LANES
    table = np.full((2, TILE, LANES), -1, np.int32)
    for way, layers in enumerate((layers_to_next(LANES), layers_to_previous(0))):
        for g in range(groups):
            for n, (c, own, there) in enumerate(layers):
                lane = g * LAYERS + n
                table[way, :4, lane] = c, own, there % LANES, g
    return table


def lane_of(shape):
    return lax.broadcasted_iota(jnp.int32, shape, len(shape) - 1)


def row_of(shape):
    return lax.broadcasted_iota(jnp.int32, shape, len(shape) - 2)


def own_field(refs, c, z):
    fe, fh, ae, ah, material = refs
    if c == KAPPA:
        return (material[z] + 1).astype(F32).astype(BF16)
    return (fe, fh, ae, ah)[c // 3][c % 3, z]


def place_on(axis):
    return lax.axis_index(axis), lax.rem(lax.axis_index(axis), 2)


def pack_kernel(x_messages, *refs):
    whole, (picker, table), refs = refs[:5], refs[5:7], refs[7:]
    fields, refs = refs[:5], refs[5:]
    x_out, xz_out = refs[:x_messages], refs[x_messages:2 * x_messages]
    z_out, ya_out, yb_low_out, yb_high_out, arrived = refs[2 * x_messages:]
    depth, rows, cols = fields[4].shape
    odd_x, odd_y, odd_z = (place_on(axis)[1] for axis in ("gx", "gy", "gz"))
    groups = depth // TILE

    copies = []
    for group in range(groups):
        planes = pl.ds(group * TILE, TILE)
        parts = [(n, slice(None), planes) for n in range(4)] + [(4, planes)]
        copies.append([
            pltpu.make_async_copy(
                whole[n].at[at], fields[n].at[at], arrived.at[group, number]
            )
            for number, (n, *at) in enumerate((p[0], *p[1:]) for p in parts)
            for at in [tuple(at)]
        ])
    for group in copies:
        for copy in group:
            copy.start()

    totals = [jnp.zeros((TILE * rows, LANES), F32)] * x_messages
    for group in range(groups):
        for copy in copies[group]:
            copy.wait()
        for z in range(group * TILE, (group + 1) * TILE):
            stacked = jnp.concatenate([own_field(fields, c, z) for c in range(COUNT)], axis=0)
            picked = jnp.dot(picker[odd_y], stacked, preferred_element_type=F32)
            ya_out[z] = picked[:LAYERS]
            half = yb_low_out.shape[0]
            if z < half:
                yb_low_out[z] = picked[LAYERS:]
            else:
                yb_high_out[z - half] = picked[LAYERS:]

        for number in range(x_messages):
            way = odd_x ^ number
            offset = pl.multiple_of((1 - way) * (cols - LANES), LANES)
            of_field, of_lane, of_group = (table[way, k:k + 1, :] for k in (0, 1, 3))
            chosen = (row_of((LANES, LANES)) == of_lane) & (of_group == group)
            planes = pl.ds(group * TILE, TILE)
            for c in range(COUNT):
                if c == KAPPA:
                    part = fields[4][planes, :, pl.ds(offset, LANES)]
                    part = (part + 1).astype(F32).astype(BF16)
                else:
                    part = fields[c // 3][c % 3, planes, :, pl.ds(offset, LANES)]
                matrix = jnp.where(chosen & (of_field == c), 1.0, 0.0).astype(BF16)
                totals[number] += jnp.dot(
                    part.reshape(TILE * rows, LANES), matrix, preferred_element_type=F32
                )

    edge = jnp.where(odd_z == 0, TILE - WIDE, 0)
    for total, out, part in zip(totals, x_out, xz_out):
        out[...] = total.reshape(TILE, rows, LANES)
        part[...] = out[pl.ds(edge, WIDE)]

    def edges(layers):
        for n, (c, own, _) in enumerate(layers):
            z_out[n] = own_field(fields, c, own).astype(F32)

    @pl.when(odd_z == 0)
    def _():
        edges(planes_to_next(depth))

    @pl.when(odd_z == 1)
    def _():
        edges(planes_to_previous(depth))


def edge_rows(array, to_next):
    rows = array.shape[0]
    row = row_of((TILE, LANES))
    last = pltpu.roll(array[rows - TILE:], SHIFT, 0)
    first = pltpu.roll(array[:TILE], SHIFT, 0)
    last = jnp.where((row >= SHIFT - WIDE) & (row < SHIFT), last, 0.0)
    first = jnp.where((row >= SHIFT) & (row < SHIFT + WIDE), first, 0.0)
    return jnp.where(to_next == 1, last, first)


def corner_kernel(x_messages, *refs):
    arrays = refs[:2 * x_messages]
    zr, picker, _, a_out, b_out = refs[2 * x_messages:]
    sent, rows, cols = zr.shape
    odd_y = place_on("gy")[1]
    arrived = zr[...].reshape(sent * rows, cols).astype(BF16)
    rest = jnp.zeros(((LAYERS - sent) * rows, cols), BF16)
    arrived = jnp.concatenate([arrived, rest], axis=0)
    picked = [
        jnp.dot(picker[odd_y], arrived[n:n + LANES], preferred_element_type=F32)
        for n in range(0, LAYERS * rows, LANES)
    ]
    count = picker.shape[1] // 2
    for message, out in ((0, a_out), (1, b_out)):
        at = 0
        for t in range(cols // LANES):
            for group in picked:
                for n in range(message * count, (message + 1) * count, TILE):
                    out[at] = lane_tile(group[n:n + TILE], t)
                    at += 1
        for array in arrays:
            for k in range(array.shape[0]):
                out[at + k] = edge_rows(array[k], 1 - (odd_y ^ message))
            at += array.shape[0]


def spread(tiles, halo):
    low = row_of((TILE, LANES)) < SHIFT
    turned = [pltpu.roll(t, SHIFT, 0) for t in tiles]
    out = [jnp.where(low, halo, turned[0])]
    for before, after in zip(turned, turned[1:]):
        out.append(jnp.where(low, before, after))
    out.append(jnp.where(low, turned[-1], halo))
    return out


def gather(tiles):
    low = row_of((TILE, LANES)) < SHIFT
    turned = [pltpu.roll(t, SHIFT, 0) for t in tiles]
    return [jnp.where(low, before, after) for before, after in zip(turned, turned[1:])]


def planes_at_once(count):
    return max(n for n in range(1, 18) if count % n == 0)


def lane_tile(array, t):
    return array[:, t * LANES:(t + 1) * LANES]


def row_tiles(array):
    return [array[b:b + TILE] for b in range(0, array.shape[0], TILE)]


def rows_at(b):
    return pl.ds(b * TILE, TILE)


def weight(number, inverse):
    value = jnp.zeros(number.shape, F32)
    for m in range(inverse.shape[0]):
        value = jnp.where(number == m + 1, inverse[m] * (COURANT * COURANT), value)
    return value


def arrange(c, own_tiles, halo, inverse):
    if c == KAPPA:
        own_tiles = [weight(p, inverse) for p in own_tiles]
        halo = weight(halo, inverse)
    elif SCALE[c] != 1.0:
        own_tiles = [p * SCALE[c] for p in own_tiles]
        halo = halo * SCALE[c]
    return spread(own_tiles, halo)


def prepare_kernel(inverse, fe, fh, ae, ah, material, table, _, matrices, *state):
    depth, _, cols = material.shape
    refs = (fe, fh, ae, ah, material)
    zero = jnp.zeros((TILE, LANES), F32)

    def planes(step, _):
        for k in range(4):
            z = step * 4 + k
            for c in range(COUNT):
                whole = own_field(refs, c, z).astype(F32)
                for t in range(cols // LANES):
                    parts = arrange(c, row_tiles(lane_tile(whole, t)), zero, inverse)
                    for b, part in enumerate(parts):
                        state[c // 3][c % 3, BEFORE + z, t, rows_at(b)] = part
        return 0

    lax.fori_loop(0, depth // 4, planes, 0)
    column_matrices(table, place_on("gx")[1], matrices)


def column_matrices(table, odd_x, out):
    target = row_of((LANES, LANES))
    for number in range(out.shape[0]):
        way = 1 - (odd_x ^ number)
        of_field, of_target, of_group = (table[way, k:k + 1, :] for k in (0, 2, 3))
        lands = of_target == target
        for c in range(COUNT):
            for pair in range(out.shape[2]):
                for n in range(2):
                    chosen = jnp.where((of_field == c) & (of_group == 2 * pair + n), SCALE[c], 0.0)
                    matrix = jnp.where(lands, chosen, 0.0).astype(BF16)
                    out[number, c, pair, n * LANES:(n + 1) * LANES] = matrix


def columns_of(matrices, c, arrays, inverse, pick):
    total = None
    for number, array in enumerate(arrays):
        part = lax.dot_general(
            array, pick(matrices, number, c), (((1,), (1,)), ((), ())), preferred_element_type=F32
        )
        total = part if total is None else total + part
    return weight(total, inverse) if c == KAPPA else total


def place_columns(matrices, own_arrays, halo_arrays, inverse, depth, odd_z, put):
    groups = depth // TILE
    begin_halo = jnp.where(odd_z == 1, BEFORE - WIDE, BEFORE + depth)
    halo_group = jnp.where(odd_z == 1, groups - 1, 0)
    half = pl.ds(pl.multiple_of(lax.rem(halo_group, 2) * LANES, LANES), LANES)
    for c in range(COUNT):
        for pair in range(groups // 2):
            found = columns_of(
                matrices, c, own_arrays, inverse, lambda m, number, c: m[number, c, pair]
            )
            for n in range(2):
                put(c, BEFORE + (2 * pair + n) * TILE, TILE, lane_tile(found, n))
        found = columns_of(
            matrices, c, halo_arrays, inverse,
            lambda m, number, c: m[number, c, halo_group // 2, half],
        )
        put(c, begin_halo, WIDE, found)


def plane_kernel(x_messages, inverse, *others):
    xp, xz = others[:x_messages], others[x_messages:2 * x_messages]
    zr, matrices = others[2 * x_messages:2 * x_messages + 2]
    state = others[2 * x_messages + 7:]
    _, rows, cols = zr.shape
    own = cols // LANES
    blocks = rows // TILE + 1
    depth = state[0].shape[1] - BEFORE - AFTER
    odd_z = place_on("gz")[1]
    zero = jnp.zeros((TILE, LANES), F32)

    for t in range(own + 1):
        for b in range(blocks):
            for c in range(3):
                for ref, slot in zip(state, (depth + BEFORE, BEFORE - 1) * 2):
                    ref[c, slot, t, rows_at(b)] = zero

    wides = []
    for array in (*xp, *xz):
        parts = []
        for k in range(array.shape[0]):
            parts += spread(row_tiles(array[k]), zero)
        wides.append(jnp.concatenate(parts, axis=0).astype(BF16))

    def put(c, slot, count, value):
        value = value.reshape(count, blocks * TILE, LANES)
        state[c // 3][c % 3, pl.ds(slot, count), own] = value

    place_columns(matrices, wides[:x_messages], wides[x_messages:], inverse, depth, odd_z, put)

    def halo_planes(layers):
        for n, (c, _, position) in enumerate(layers):
            for t in range(own):
                parts = arrange(c, row_tiles(lane_tile(zr[n], t)), zero, inverse)
                for b, part in enumerate(parts):
                    state[c // 3][c % 3, position + BEFORE, t, rows_at(b)] = part

    @pl.when(odd_z == 0)
    def _():
        halo_planes(planes_to_previous(depth))

    @pl.when(odd_z == 1)
    def _():
        halo_planes(planes_to_next(depth))


def first_slot(count, depth, odd_z):
    return BEFORE + jnp.where(odd_z == 1, depth - count, 0)


def ahead_lanes(parts):
    lane = lane_of((TILE, LANES))
    turned = [pltpu.roll(p, LANES - 1, 1) for p in parts]
    after = turned[1:] + turned[:1]
    return [jnp.where(lane == LANES - 1, a, t) for a, t in zip(after, turned)]


def reader(ref, slot):
    blocks = ref.shape[3] // TILE
    seen = {}

    def read(c, ahead, t, b):
        if (c, ahead, t, b) not in seen:
            seen[c, ahead, t, b] = ref[c, slot + ahead, t, rows_at(b)]
        return seen[c, ahead, t, b]

    def ahead_rows(c, ahead, t, b):
        if b == blocks - 1:
            return pltpu.roll(read(c, ahead, t, b), TILE - 1, 0)
        return ref[c, slot + ahead, t, pl.ds(b * TILE + 1, TILE)]

    def behind_rows(c, ahead, t, b):
        if b == 0:
            return pltpu.roll(read(c, ahead, t, b), 1, 0)
        return ref[c, slot + ahead, t, pl.ds(b * TILE - 1, TILE)]

    return read, ahead_rows, behind_rows


def magnetic_step(e, g, first, count, width, store):
    tiles, blocks = e.shape[2], e.shape[3] // TILE
    unroll = planes_at_once(count)

    def step(number, _):
        slot = first + number * unroll
        read, ahead_rows, _ = reader(e, slot)
        old, _, _ = reader(g, slot)
        results = {}
        for k in range(unroll):
            for b in range(blocks):
                y_x = ahead_lanes([read(1, k, t, b) for t in range(tiles)])
                z_x = ahead_lanes([read(2, k, t, b) for t in range(tiles)])
                for t in range(width):
                    ex, ey, ez = (read(c, k, t, b) for c in range(3))
                    curl = (
                        (ahead_rows(2, k, t, b) - ez) - (read(1, k + 1, t, b) - ey),
                        (read(0, k + 1, t, b) - ex) - (z_x[t] - ez),
                        (y_x[t] - ey) - (ahead_rows(0, k, t, b) - ex),
                    )
                    for c in range(3):
                        results[c, k, t, b] = old(c, k, t, b) + curl[c]
        store(slot, results)
        return 0

    lax.fori_loop(0, count // unroll, step, 0)


def dual_kernel(third_e, dual_g, dual_out):
    _, depth, rows, cols = dual_out.shape
    own, blocks = cols // LANES, rows // TILE + 1

    def store(slot, results):
        for c, k, t, b in results:
            if b == 0:
                values = gather([results[c, k, t, n] for n in range(blocks)])
                for n, value in enumerate(values):
                    where = (c, slot + k - BEFORE, rows_at(n), pl.ds(t * LANES, LANES))
                    dual_out[where] = value * COURANT

    magnetic_step(third_e, dual_g, BEFORE, depth, own, store)


def row_kernel(inverse, ya, yb_low, yb_high, placer, *state):
    state = state[5:]
    odd_y = place_on("gy")[1]
    own = ya.shape[2] // LANES
    height = state[0].shape[3]
    below, above = pl.ds(0, SHIFT), pl.ds(height - SHIFT, SHIFT)
    at_once = 8

    def place(array, start):
        def step(number, _):
            results = []
            for k in range(at_once):
                z = number * at_once + k
                arrived = jnp.concatenate([ya[start + z], array[z]], axis=0).astype(BF16)
                results.append(jnp.dot(placer[odd_y], arrived, preferred_element_type=F32))
            for k, halos in enumerate(results):
                z = number * at_once + k + start
                for c in range(COUNT):
                    for t in range(own):
                        halo = lane_tile(halos[c * TILE:(c + 1) * TILE], t)
                        if c == KAPPA:
                            halo = weight(halo, inverse)
                        at = (c % 3, z + BEFORE, t)
                        state[c // 3][(*at, below)] = halo[:SHIFT]
                        state[c // 3][(*at, above)] = halo[SHIFT:]
            return 0

        lax.fori_loop(0, array.shape[0] // at_once, step, 0)

    place(yb_low, 0)
    place(yb_high, yb_low.shape[0])


def window_kernel(x_messages, inverse, height, *others):
    corner_a, corner_b, corner_placing, matrices = others[:4]
    grad_out, forward_e, forward_g, dual_e, dual_g, factor, third_e, second_e = others[9:]
    rows, cols = height.shape
    depth = factor.shape[1] - BEFORE - AFTER
    own = cols // LANES
    tiles = own + 1
    blocks = rows // TILE + 1
    (at_x, odd_x), (at_y, odd_y), (at_z, odd_z) = (place_on(axis) for axis in ("gx", "gy", "gz"))
    start_z = at_z * depth
    row = row_of((TILE, LANES))
    lane = lane_of((TILE, LANES))
    zero = jnp.zeros((TILE, LANES), F32)
    state = (forward_e, forward_g, dual_e, dual_g, factor)
    below, above = pl.ds(0, SHIFT), pl.ds(blocks * TILE - SHIFT, SHIFT)

    for t in range(tiles):
        for b in range(blocks):
            for c in range(3):
                second_e[c, depth + BEFORE, t, rows_at(b)] = zero
                third_e[c, depth + BEFORE, t, rows_at(b)] = zero

    corner_tiles = LAYERS * WIDE // TILE
    at = own * corner_tiles
    wides = []
    for count in [TILE] * x_messages + [WIDE] * x_messages:
        parts = [corner_a[at + k] + corner_b[at + k] for k in range(count)]
        wides.append(jnp.concatenate(parts, axis=0).astype(BF16))
        at += count

    def put(c, slot, count, value):
        value = value.reshape(count, TILE, LANES)
        slots = pl.ds(slot, count)
        state[c // 3][c % 3, slots, own, below] = value[:, :SHIFT]
        state[c // 3][c % 3, slots, own, above] = value[:, SHIFT:]

    place_columns(matrices, wides[:x_messages], wides[x_messages:], inverse, depth, odd_z, put)

    group = LANES // rows
    group_tiles = group * WIDE // TILE
    plane_halos = []
    for n in range(LAYERS // group):
        arrived = jnp.concatenate([
            jnp.concatenate([ref[t * corner_tiles + k] for t in range(own)], axis=1)
            for ref in (corner_a, corner_b) for k in range(n * group_tiles, (n + 1) * group_tiles)
        ], axis=0).astype(BF16)
        placed = jnp.dot(corner_placing[odd_y], arrived, preferred_element_type=F32)
        plane_halos += [placed[k * TILE:(k + 1) * TILE] for k in range(group)]

    def halo_planes(layers):
        for n, (c, _, position) in enumerate(layers):
            for t in range(own):
                halo = lane_tile(plane_halos[n], t) * SCALE[c]
                if c == KAPPA:
                    halo = weight(halo, inverse)
                at = (c % 3, position + BEFORE, t)
                state[c // 3][(*at, below)] = halo[:SHIFT]
                state[c // 3][(*at, above)] = halo[SHIFT:]

    @pl.when(odd_z == 0)
    def _():
        halo_planes(planes_to_previous(depth))

    @pl.when(odd_z == 1)
    def _():
        halo_planes(planes_to_next(depth))

    keep_row = jnp.where((row < SHIFT) & (at_y == 0), 0.0, 1.0)
    keep_lane = jnp.where((lane >= LANES // 2) & (at_x == 0), 0.0, 1.0)

    def mask(value, t, b):
        if b == 0:
            value = value * keep_row
        if t == own:
            value = value * keep_lane
        return value

    def behind_lanes(parts):
        turned = [pltpu.roll(p, 1, 1) for p in parts]
        return [jnp.where(lane == 0, turned[(t - 1) % tiles], turned[t]) for t in range(tiles)]

    def begin(count):
        return first_slot(count, depth, odd_z)

    def magnetic(e, g, count):
        def store(slot, results):
            for (c, k, t, b), value in results.items():
                g[c, slot + k, t, rows_at(b)] = mask(value, t, b)

        magnetic_step(e, g, begin(count), count, tiles, store)

    def electric(e, g, to, count, partner=None, totals=()):
        unroll = planes_at_once(count)
        first = begin(count)

        def step(number, carry):
            carry = list(carry)
            slot = first + number * unroll
            read, _, behind_rows = reader(g, slot)
            old, _, _ = reader(e, slot)
            weights, _, _ = reader(factor, slot)
            results = {}
            for k in range(unroll):
                if partner is not None:
                    position = slot + k - BEFORE
                    inside = (position >= 0) & (position < depth)
                    position = jnp.where(inside, position + start_z, jnp.int32(2**30))
                for b in range(blocks):
                    y_x = behind_lanes([read(1, k, t, b) for t in range(tiles)])
                    z_x = behind_lanes([read(2, k, t, b) for t in range(tiles)])
                    for t in range(tiles):
                        gx, gy, gz = (read(c, k, t, b) for c in range(3))
                        curl = (
                            (gz - behind_rows(2, k, t, b)) - (gy - read(1, k - 1, t, b)),
                            (gx - read(0, k - 1, t, b)) - (gz - z_x[t]),
                            (gy - y_x[t]) - (gx - behind_rows(0, k, t, b)),
                        )
                        scale = weights(0, k, t, b)
                        product = None
                        for c in range(3):
                            value = old(c, k, t, b) - scale * curl[c]
                            results[c, k, t, b] = value
                            if partner is not None and t < own:
                                term = value * partner[c, slot + k, t, rows_at(b)]
                                product = term if product is None else product + term
                        if product is not None:
                            chosen = position < limits[t * blocks + b]
                            carry[t * blocks + b] += jnp.where(chosen, product, 0.0)
            for (c, k, t, b), value in results.items():
                to[c, slot + k, t, rows_at(b)] = value
            return tuple(carry)

        return lax.fori_loop(0, count // unroll, step, totals)

    def count(low, high):
        planes = depth + max(low, high)
        return planes if planes_at_once(planes) > 8 else planes + 1

    magnetic(dual_e, dual_g, count(2, 2))
    electric(dual_e, dual_g, second_e, count(1, 2))
    magnetic(second_e, dual_g, count(1, 1))
    electric(second_e, dual_g, third_e, count(0, 1))

    none = jnp.zeros((TILE, LANES), jnp.int32)
    limits = []
    for t in range(own):
        limits += spread(row_tiles(lane_tile(height[...], t)), none)
    totals = (zero,) * (own * blocks)
    magnetic(forward_e, forward_g, count(3, 2))
    totals = electric(forward_e, forward_g, forward_e, count(2, 2), third_e, totals)
    magnetic(forward_e, forward_g, count(2, 1))
    totals = electric(forward_e, forward_g, forward_e, count(1, 1), second_e, totals)
    magnetic(forward_e, forward_g, count(1, 0))
    totals = electric(forward_e, forward_g, forward_e, depth, dual_e, totals)
    for t in range(own):
        values = gather(list(totals[t * blocks:(t + 1) * blocks]))
        for b, value in enumerate(values):
            grad_out[rows_at(b), t * LANES:(t + 1) * LANES] = value


def corner_swap(array, axes, offsets):
    lengths = [lax.axis_size(a) for a in axes]
    pairs = [
        (i * lengths[1] + j, k * lengths[1] + l)
        for i, k in swap_pairs(lengths[0], offsets[0])
        for j, l in swap_pairs(lengths[1], offsets[1])
    ]
    return lax.ppermute(array, axes, pairs)


def local(forward_e, forward_h, adjoint_e, adjoint_h, material, inv_permittivity, height):
    depth, rows, cols = material.shape
    tiles = cols // LANES
    nx, nz = lax.axis_size("gx"), lax.axis_size("gz")
    assert nz == 2
    picker = jnp.asarray(row_picker(rows), BF16)
    placer = jnp.asarray(row_placer(rows), BF16)
    corner_picking = jnp.asarray(corner_picker(rows), BF16)
    corner_placing = jnp.asarray(corner_placer(rows), BF16)
    table = jnp.asarray(column_table(depth))
    vmem = pl.BlockSpec(memory_space=pltpu.VMEM)
    smem = pl.BlockSpec(memory_space=pltpu.SMEM)
    params = pltpu.CompilerParams(vmem_limit_bytes=24 * 1024 * 1024)
    anywhere = pl.BlockSpec(memory_space=pl.ANY)
    x_messages = 1 if nx == 2 else 2

    chunk = TILE
    x_shape = pltpu.VMEM((chunk, rows, LANES), F32)
    xz_shape = pltpu.VMEM((WIDE, rows, LANES), F32)
    y_shape = pltpu.VMEM((depth, LAYERS, cols), F32)
    fields = (forward_e, forward_h, adjoint_e, adjoint_h, material)
    in_hbm = pl.BlockSpec(memory_space=pltpu.HBM)
    half_shape = pltpu.VMEM((depth // 2, LAYERS, cols), F32)
    packed = pl.pallas_call(
        functools.partial(pack_kernel, x_messages),
        out_shape=[pltpu.VMEM(f.shape, f.dtype) for f in fields]
        + [x_shape] * x_messages + [xz_shape] * x_messages
        + [pltpu.VMEM((len(planes_to_next(depth)), rows, cols), F32), y_shape, half_shape, half_shape],
        in_specs=[in_hbm] * 5 + [vmem] * 2,
        out_specs=[vmem] * (2 * x_messages + 9),
        scratch_shapes=[pltpu.SemaphoreType.DMA((depth // TILE, 5))],
        compiler_params=pltpu.CompilerParams(vmem_limit_bytes=54 * 1024 * 1024),
        name="pack",
    )(*fields, picker, table)
    fields, packed = packed[:5], packed[5:]
    z_message, ya, yb_low, yb_high = packed[2 * x_messages:]
    ya = swap(ya, "gy", 0)
    zr = swap(z_message, "gz", 0)
    yb_low = swap(yb_low, "gy", 1)
    yb_high = swap(yb_high, "gy", 1)
    xp = [swap(packed[n], "gx", n) for n in range(x_messages)]
    xz = [corner_swap(packed[x_messages + n], ("gx", "gz"), (n, 0)) for n in range(x_messages)]

    block = (BEFORE + depth + AFTER, tiles + 1, (rows // TILE + 1) * TILE, LANES)
    state_shapes = [pltpu.VMEM((3,) + block, F32)] * 4 + [pltpu.VMEM((1,) + block, F32)]
    matrix_shape = pltpu.VMEM((x_messages, COUNT, depth // TILE // 2, 2 * LANES, LANES), BF16)
    matrices, *state = pl.pallas_call(
        prepare_kernel,
        out_shape=[matrix_shape] + state_shapes,
        in_specs=[smem] + [vmem] * 6 + [anywhere],
        out_specs=[vmem] * 6,
        compiler_params=pltpu.CompilerParams(vmem_limit_bytes=8 * 1024 * 1024),
        name="prepare",
    )(inv_permittivity, *fields, table, ya)

    corner_tiles = LAYERS * WIDE // TILE * tiles + x_messages * (chunk + WIDE)
    corner_shape = jax.ShapeDtypeStruct((corner_tiles, TILE, LANES), F32)
    corner_a, corner_b = pl.pallas_call(
        functools.partial(corner_kernel, x_messages),
        out_shape=[corner_shape, corner_shape],
        in_specs=[vmem] * (2 * x_messages + 2) + [anywhere],
        out_specs=[vmem] * 2,
        compiler_params=pltpu.CompilerParams(vmem_limit_bytes=8 * 1024 * 1024),
        name="corners",
    )(*xp, *xz, zr, corner_picking, state[4])
    corner_b = swap(corner_b, "gy", 1)
    corner_a = swap(corner_a, "gy", 0)

    operands = (inv_permittivity, *xp, *xz, zr, matrices)
    state = pl.pallas_call(
        functools.partial(plane_kernel, x_messages),
        out_shape=state_shapes,
        in_specs=[smem] + [vmem] * (len(operands) + 4),
        out_specs=[vmem] * 5,
        input_output_aliases={len(operands) + n: n for n in range(5)},
        compiler_params=pltpu.CompilerParams(vmem_limit_bytes=8 * 1024 * 1024),
        name="planes",
    )(*operands, *state)

    operands = (inv_permittivity, ya, yb_low, yb_high, placer)
    state = pl.pallas_call(
        row_kernel,
        out_shape=state_shapes,
        in_specs=[smem] + [vmem] * (len(operands) + 4),
        out_specs=[vmem] * 5,
        input_output_aliases={len(operands) + n: n for n in range(5)},
        compiler_params=pltpu.CompilerParams(vmem_limit_bytes=8 * 1024 * 1024),
        name="rows",
    )(*operands, *state)

    operands = (inv_permittivity, height, corner_a, corner_b, corner_placing, matrices)
    results = pl.pallas_call(
        functools.partial(window_kernel, x_messages),
        out_shape=[jax.ShapeDtypeStruct((rows, cols), F32), *state_shapes, state_shapes[0]],
        in_specs=[smem] + [vmem] * (len(operands) + 4),
        out_specs=[vmem] * 7,
        input_output_aliases={len(operands) + n: 1 + n for n in range(5)},
        scratch_shapes=[pltpu.VMEM((3,) + block, F32)],
        compiler_params=pltpu.CompilerParams(vmem_limit_bytes=16 * 1024 * 1024),
        name="window",
    )(*operands, *state)
    grad, dual_g, third_e = results[0], results[4], results[6]
    dual = pl.pallas_call(
        dual_kernel,
        out_shape=jax.ShapeDtypeStruct((3, depth, rows, cols), F32),
        in_specs=[vmem] * 2,
        out_specs=vmem,
        compiler_params=pltpu.CompilerParams(vmem_limit_bytes=8 * 1024 * 1024),
        name="dual",
    )(third_e, dual_g)
    return grad + swap(grad, "gz", 0), dual


def solution(mesh):
    fields = P(None, "gz", "gy", "gx")
    return jax.shard_map(
        local,
        mesh=mesh,
        in_specs=(fields, fields, fields, fields, P("gz", "gy", "gx"), P(), P("gy", "gx")),
        out_specs=(P("gy", "gx"), fields),
        check_vma=False,
    )
```
